32 devices in a mesh: seq: 16 (over z, y, core), samp: 2 (over x).
Axes of the slice: x: 2, y: 2, z: 4, core: 2. Of those that a mesh axis runs over, the one named last changes fastest.
Arguments:
- trunk: bfloat16 [2, 4096, 768], P('samp', 'seq'), may hold values from -6 to 6
- conv_weight: bfloat16 [3, 3, 768, 768], replicated, may hold values from -0.125 to 0.125
- head_weight: bfloat16 [768, 2688], replicated, may hold values from -0.21875 to 0.21875
- targets: int32 [2, 4096, 2688], P('samp', 'seq'), may hold values from 0 to 8
- error_mask: int32 [2, 4096], P('samp', 'seq'), may hold values 0 or 1
- upweight: int32 [2, 4096], P('samp', 'seq'), may hold values from 1 to 16, as said below
Outputs:
- loss: float32 [], replicated
- grad_conv: float32 [3, 2304, 768], P(None, 'seq', 'samp')
- grad_head: float32 [768, 2688], P('seq', 'samp')
- trunk_input_gradient: bfloat16 [2, 4096, 768], P('samp', 'seq')
The draws below stay inside these ranges and needn't reach their ends.
Inputs may be any that keep to these rules, and one draw needn't show every extreme that they name: upweight is 1 at the first bin of each window and 16 at the last; at bin p it is at most 1 + (15 p) // 4095.
All inputs are finite; a program needn't handle non-finite values. No bound on the sum of `error_mask` on one device may be relied on, other than what follows from the above.
Results may differ from the reference program's by a relative error of at most 0.015.
Values may be sent and summed in bfloat16 or wider, within the bound.
A program may use at most 192 MiB of HBM per device.

```python
import jax
import jax.numpy as jnp
from jax import lax

C = 768
OUTPUT_TRACKS = 2688
LAYERS = 3
BASE_DILATION = 64
LENGTH = 4096
BATCH = 2


def draw_upweight(key, part):
    places = jnp.arange(LENGTH, dtype=jnp.int32)
    ceiling = 2 + 15 * places // max(LENGTH - 1, 1)
    drawn = jax.random.randint(key, (BATCH, LENGTH), 1, ceiling[None, :])
    drawn = jnp.where(places[None, :] == LENGTH - 1, 16, drawn)
    return drawn.astype(jnp.int32)


def touch_ends(entries, key, smallest, high):
    place = [jax.random.randint(jax.random.fold_in(key, axis), (), 0, length) for axis, length in enumerate(entries.shape)]
    longest = entries.shape.index(max(entries.shape))
    next_to = place[:longest] + [(place[longest] + 1) % entries.shape[longest]] + place[longest + 1:]
    return entries.at[tuple(place)].set(smallest).at[tuple(next_to)].set(high)


def block_levels(key, shape, shards, least, largest):
    def one(dim, blocks):
        steps = jax.random.uniform(jax.random.fold_in(jax.random.fold_in(key, 6), dim), (blocks,), jnp.float32, least / len(shards), largest / len(shards))
        return jnp.repeat(jnp.exp(steps), shape[dim] // blocks).reshape((-1,) + (1,) * (len(shape) - dim - 1))

    gain = one(*shards[0])
    for cut in shards[1:]:
        gain = gain * one(*cut)
    return gain


def bell_draw(rng, shape, deviation, limit, cuts=(), kind=jnp.bfloat16):
    gain = block_levels(rng, shape, cuts, -0.22, 0.18) if cuts else 1.0
    result = jax.random.normal(rng, shape, jnp.float32) * deviation * gain
    return jnp.minimum(jnp.maximum(result, -limit), limit).astype(kind)


def setup_inputs(seed: int = 0) -> dict:
    streams_of = jax.random.split(jax.random.key(seed), 7)
    trunk = bell_draw(streams_of[0], (BATCH, LENGTH, C), 1.0, 6.0, ((0, 2), (1, 16)))
    conv_weight = bell_draw(streams_of[1], (LAYERS, 3, C, C), (3 * C) ** -0.5, 0.125)
    head_weight = bell_draw(streams_of[2], (C, OUTPUT_TRACKS), C ** -0.5, 0.21875)
    targets = touch_ends(jax.random.randint(streams_of[3], (BATCH, LENGTH, OUTPUT_TRACKS), 0, 9), jax.random.fold_in(streams_of[3], 1), 0, 8).astype(jnp.int32)
    error_mask = touch_ends((jax.random.randint(streams_of[4], (BATCH, LENGTH), 0, 2) < 1).astype(jnp.int32), jax.random.fold_in(streams_of[4], 1), 0, 1)
    upweight = draw_upweight(jax.random.fold_in(streams_of[6], 71), 0)
    return {"trunk": trunk, "conv_weight": conv_weight, "head_weight": head_weight, "targets": targets, "error_mask": error_mask, "upweight": upweight}


def smooth(values):
    return jax.nn.gelu(values, approximate=True)

def shifted(values, offset):
    length_all = values.shape[1]
    margin = abs(offset)
    padded = jnp.pad(values, ((0, 0), (margin, margin), (0, 0)))
    return padded[:, margin + offset:margin + offset + length_all]

def reference(trunk, conv_weight, head_weight, targets, error_mask, upweight):
    bin_weight = jnp.where(error_mask == 1, upweight, 1).astype(jnp.float32)
    weight_sum = jnp.sum(bin_weight)
    factor = BATCH * LENGTH / weight_sum
    stream = trunk
    stored = []
    activations = []
    for layer_number in range(LAYERS):
        dilation_spread = BASE_DILATION * 2 ** layer_number
        activated = smooth(stream.astype(jnp.float32)).astype(jnp.bfloat16)
        conv_out = jnp.zeros((BATCH * LENGTH, C), jnp.float32)
        for tap_num in range(3):
            moved = shifted(activated, (tap_num - 1) * dilation_spread).reshape(-1, C)
            conv_out = conv_out + jnp.dot(moved, conv_weight[layer_number, tap_num], preferred_element_type=jnp.float32)
        stored.append(stream)
        activations.append(activated)
        stream = (stream.astype(jnp.float32) + conv_out.reshape(stream.shape)).astype(jnp.bfloat16)

    def head_part(inputs):
        window_rows, window_counts, window_weight = inputs
        logits = jnp.dot(window_rows, head_weight, preferred_element_type=jnp.float32)
        predicted = jax.nn.softplus(logits)
        slope = jax.nn.sigmoid(logits)
        counts = window_counts.astype(jnp.float32)
        partial_loss = jnp.sum(window_weight[:, None] * (predicted - counts * jnp.log(predicted)))
        logit_grad = (factor * window_weight[:, None] * (1.0 - counts / predicted) * slope).astype(jnp.bfloat16)
        head_grad = jnp.dot(window_rows.T, logit_grad, preferred_element_type=jnp.float32)
        back_grad = jnp.dot(logit_grad, head_weight.T, preferred_element_type=jnp.float32)
        return (partial_loss, back_grad, head_grad)
    loss_parts, stream_grad, head_grads = lax.map(head_part, (stream, targets, bin_weight))
    loss = jnp.sum(loss_parts) / (OUTPUT_TRACKS * weight_sum)
    grad_head = lax.optimization_barrier(jnp.sum(head_grads, axis=0))
    kernel_grads = [None] * LAYERS
    for layer_number in reversed(range(LAYERS)):
        dilation_spread = BASE_DILATION * 2 ** layer_number
        grad_bf = stream_grad.astype(jnp.bfloat16)
        grad_flat = grad_bf.reshape(-1, C)
        pieces = []
        act_grad = jnp.zeros((BATCH * LENGTH, C), jnp.float32)
        for tap_num in range(3):
            offset = (tap_num - 1) * dilation_spread
            moved = shifted(activations[layer_number], offset).reshape(-1, C)
            pieces.append(jnp.dot(moved.T, grad_flat, preferred_element_type=jnp.float32))
            back_moved = shifted(grad_bf, -offset).reshape(-1, C)
            act_grad = act_grad + jnp.dot(back_moved, conv_weight[layer_number, tap_num].T, preferred_element_type=jnp.float32)
        kernel_grads[layer_number] = jnp.concatenate(pieces, axis=0)
        residual_float32 = stored[layer_number].astype(jnp.float32)
        pullback = jax.vjp(smooth, residual_float32)[1]
        stream_grad = stream_grad + pullback(act_grad.reshape(residual_float32.shape))[0]
    grad_conv = jnp.stack(kernel_grads, axis=0)
    return (loss, grad_conv, grad_head, stream_grad.astype(jnp.bfloat16))
```

```python
import jax
import jax.numpy as jnp
from jax import lax
from jax.sharding import PartitionSpec as P

OUTPUT_TRACKS = 2688
LAYERS = 3
BASE_DILATION = 64


def extended(shard, width):
    devices, length = (lax.axis_size("seq"), shard.shape[1])
    up = [(i, (i + 1) % devices) for i in range(devices - 1)]
    down = [(j, i) for i, j in up]
    before = lax.ppermute(lax.slice_in_dim(shard, length - width, length, axis=1), "seq", up)
    after = lax.ppermute(lax.slice_in_dim(shard, 0, width, axis=1), "seq", down)
    return jnp.concatenate([before, shard, after], axis=1)


def smooth(values):
    return jax.nn.gelu(values, approximate=True)


def halve(part, dim, axis, bit):
    place = lax.axis_index(axis)
    mine = lax.rem(lax.div(place, 2**bit), 2)
    pairs = [(i, i ^ (2**bit)) for i in range(lax.axis_size(axis))]
    away = lax.dynamic_index_in_dim(part, 1 - mine, dim, keepdims=False)
    kept = lax.dynamic_index_in_dim(part, mine, dim, keepdims=False)
    come = lax.ppermute(away, axis, pairs)
    return (kept.astype(jnp.float32) + come.astype(jnp.float32)).astype(jnp.bfloat16)


def scatter_sum(part, order):
    labels = ["samp"] + list(reversed(range(part.ndim - 3)))
    for step in order:
        dim = labels.index(step)
        part = halve(part, dim, *(("samp", 0) if step == "samp" else ("seq", step)))
        labels.pop(dim)
    return part


def reduced(halves):
    devices = lax.axis_size("seq")
    bits = devices.bit_length() - 1
    rows = halves[0].shape[0] // devices
    stacked = jnp.stack([h.reshape((2,) * bits + (rows, h.shape[1])) for h in halves], axis=0)
    cut = max((rows * 5 // 9) // 16 * 16, 1)
    higher = list(range(2, bits))
    first = scatter_sum(stacked[..., :cut, :], [0, "samp", 1] + higher)
    second = scatter_sum(stacked[..., cut:, :], [0, 1, "samp"] + higher)
    return jnp.concatenate([first, second], axis=0).astype(jnp.float32)


def per_device(trunk, conv_weight, head_weight, targets, error_mask, upweight):
    windows, positions, channels = trunk.shape
    row_count = windows * positions
    bins_all = row_count * lax.axis_size("seq") * lax.axis_size("samp")
    bin_weight = jnp.where(error_mask == 1, upweight, 1).astype(jnp.float32)
    weight_sum = lax.psum(jnp.sum(bin_weight), ("seq", "samp"))
    stream = trunk
    stored = []
    padded_acts = []
    for layer_number in range(LAYERS):
        spread = BASE_DILATION * 2**layer_number
        activated = smooth(stream.astype(jnp.float32)).astype(jnp.bfloat16)
        padded = extended(activated, spread)
        taps = jnp.concatenate(
            [padded[:, k * spread : k * spread + positions] for k in range(3)], axis=2
        ).reshape(row_count, 3 * channels)
        conv_out = jnp.dot(
            taps,
            conv_weight[layer_number].reshape(3 * channels, channels),
            preferred_element_type=jnp.float32,
        )
        stored.append(stream)
        padded_acts.append(taps)
        stream = (stream.astype(jnp.float32) + conv_out.reshape(stream.shape)).astype(jnp.bfloat16)
    residual_rows = stream.reshape(row_count, channels)
    logits = jnp.dot(residual_rows, head_weight, preferred_element_type=jnp.float32)
    predicted = jax.nn.softplus(logits)
    slope = jax.nn.sigmoid(logits)
    counts = targets.reshape(row_count, -1).astype(jnp.float32)
    flat_weight = bin_weight.reshape(row_count, 1)
    partial_loss = jnp.sum(flat_weight * (predicted - counts * jnp.log(predicted)))
    loss_sum = lax.psum(partial_loss, ("seq", "samp"))
    factor = bins_all / weight_sum
    logit_grad = (factor * flat_weight * (1.0 - counts / predicted) * slope).astype(jnp.bfloat16)
    half = logit_grad.shape[1] // 2
    head_total = reduced(
        [
            jnp.dot(residual_rows.T, part, preferred_element_type=jnp.float32).astype(jnp.bfloat16)
            for part in (logit_grad[:, :half], logit_grad[:, half:])
        ]
    )
    stream_grad = jnp.dot(logit_grad, head_weight.T, preferred_element_type=jnp.float32).reshape(
        windows, positions, channels
    )
    kernel_grads = [None] * LAYERS
    for layer_number in reversed(range(LAYERS)):
        spread = BASE_DILATION * 2**layer_number
        grad_bf = stream_grad.astype(jnp.bfloat16)
        grad_flat = grad_bf.reshape(row_count, channels)
        padded_grad = extended(grad_bf, spread)
        side = channels // 2
        kernel_grads[layer_number] = reduced(
            [
                jnp.dot(
                    padded_acts[layer_number].T, part, preferred_element_type=jnp.float32
                ).astype(jnp.bfloat16)
                for part in (grad_flat[:, :side], grad_flat[:, side:])
            ]
        )
        act_grad = jnp.zeros((row_count, channels), jnp.float32)
        for k in range(3):
            view = padded_grad[:, (2 - k) * spread : (2 - k) * spread + positions]
            act_grad = act_grad + jnp.dot(
                view.reshape(row_count, channels),
                conv_weight[layer_number, k].T,
                preferred_element_type=jnp.float32,
            )
        residual_float32 = stored[layer_number].astype(jnp.float32)
        pullback = jax.vjp(smooth, residual_float32)[1]
        stream_grad = stream_grad + pullback(act_grad.reshape(residual_float32.shape))[0]
    loss = loss_sum / (OUTPUT_TRACKS * weight_sum)
    return (loss, jnp.stack(kernel_grads), head_total, stream_grad.astype(jnp.bfloat16))


def solution(mesh):
    return jax.shard_map(
        per_device,
        mesh=mesh,
        in_specs=(
            P("samp", "seq", None),
            P(),
            P(),
            P("samp", "seq", None),
            P("samp", "seq"),
            P("samp", "seq"),
        ),
        out_specs=(P(), P(None, "seq", "samp"), P("seq", "samp"), P("samp", "seq", None)),
        check_vma=False,
    )
```

```python
import functools

import jax
import jax.numpy as jnp
from jax import lax
from jax.experimental import pallas as pl
from jax.experimental.pallas import tpu as pltpu
from jax.sharding import PartitionSpec as P

OUTPUT_TRACKS = 2688
LAYERS = 3
BASE_DILATION = 64


def extended(shard, width):
    devices, length = (lax.axis_size("seq"), shard.shape[1])
    up = [(i, (i + 1) % devices) for i in range(devices - 1)]
    down = [(j, i) for i, j in up]
    before = lax.ppermute(lax.slice_in_dim(shard, length - width, length, axis=1), "seq", up)
    after = lax.ppermute(lax.slice_in_dim(shard, 0, width, axis=1), "seq", down)
    return jnp.concatenate([before, shard, after], axis=1)


def smooth(values):
    return jax.nn.gelu(values, approximate=True)


def halve(part, dim, axis, bit):
    place = lax.axis_index(axis)
    mine = lax.rem(lax.div(place, 2**bit), 2)
    pairs = [(i, i ^ (2**bit)) for i in range(lax.axis_size(axis))]
    away = lax.dynamic_index_in_dim(part, 1 - mine, dim, keepdims=False)
    kept = lax.dynamic_index_in_dim(part, mine, dim, keepdims=False)
    come = lax.ppermute(away, axis, pairs)
    return (kept.astype(jnp.float32) + come.astype(jnp.float32)).astype(jnp.bfloat16)


def scatter_sum(part, order):
    labels = ["samp"] + list(reversed(range(part.ndim - 3)))
    for step in order:
        dim = labels.index(step)
        part = halve(part, dim, *(("samp", 0) if step == "samp" else ("seq", step)))
        labels.pop(dim)
    return part


def reduced(halves):
    devices = lax.axis_size("seq")
    bits = devices.bit_length() - 1
    rows = halves[0].shape[0] // devices
    stacked = jnp.stack([h.reshape((2,) * bits + (rows, h.shape[1])) for h in halves], axis=0)
    cut = max((rows * 5 // 9) // 16 * 16, 1)
    higher = list(range(2, bits))
    first = scatter_sum(stacked[..., :cut, :], [0, "samp", 1] + higher)
    second = scatter_sum(stacked[..., cut:, :], [0, 1, "samp"] + higher)
    return jnp.concatenate([first, second], axis=0).astype(jnp.float32)


def per_device(trunk, conv_weight, head_weight, targets, error_mask, upweight):
    windows, positions, channels = trunk.shape
    row_count = windows * positions
    bins_all = row_count * lax.axis_size("seq") * lax.axis_size("samp")
    bin_weight = jnp.where(error_mask == 1, upweight, 1).astype(jnp.float32)
    weight_sum = lax.psum(jnp.sum(bin_weight), ("seq", "samp"))
    stream = trunk
    stored = []
    padded_acts = []
    for layer_number in range(LAYERS):
        spread = BASE_DILATION * 2**layer_number
        activated = smooth(stream.astype(jnp.float32)).astype(jnp.bfloat16)
        padded = extended(activated, spread)
        taps = jnp.concatenate(
            [padded[:, k * spread : k * spread + positions] for k in range(3)], axis=2
        ).reshape(row_count, 3 * channels)
        conv_out = jnp.dot(
            taps,
            conv_weight[layer_number].reshape(3 * channels, channels),
            preferred_element_type=jnp.float32,
        )
        stored.append(stream)
        padded_acts.append(taps)
        stream = (stream.astype(jnp.float32) + conv_out.reshape(stream.shape)).astype(jnp.bfloat16)
    residual_rows = stream.reshape(row_count, channels)
    logits = jnp.dot(residual_rows, head_weight, preferred_element_type=jnp.float32)
    predicted = jax.nn.softplus(logits)
    slope = jax.nn.sigmoid(logits)
    counts = targets.reshape(row_count, -1).astype(jnp.float32)
    flat_weight = bin_weight.reshape(row_count, 1)
    partial_loss = jnp.sum(flat_weight * (predicted - counts * jnp.log(predicted)))
    loss_sum = lax.psum(partial_loss, ("seq", "samp"))
    factor = bins_all / weight_sum
    logit_grad = (factor * flat_weight * (1.0 - counts / predicted) * slope).astype(jnp.bfloat16)
    half = logit_grad.shape[1] // 2
    head_total = reduced(
        [
            jnp.dot(residual_rows.T, part, preferred_element_type=jnp.float32).astype(jnp.bfloat16)
            for part in (logit_grad[:, :half], logit_grad[:, half:])
        ]
    )
    stream_grad = jnp.dot(logit_grad, head_weight.T, preferred_element_type=jnp.float32).reshape(
        windows, positions, channels
    )
    kernel_grads = [None] * LAYERS
    for layer_number in reversed(range(LAYERS)):
        spread = BASE_DILATION * 2**layer_number
        grad_bf = stream_grad.astype(jnp.bfloat16)
        grad_flat = grad_bf.reshape(row_count, channels)
        padded_grad = extended(grad_bf, spread)
        side = channels // 2
        kernel_grads[layer_number] = reduced(
            [
                jnp.dot(
                    padded_acts[layer_number].T, part, preferred_element_type=jnp.float32
                ).astype(jnp.bfloat16)
                for part in (grad_flat[:, :side], grad_flat[:, side:])
            ]
        )
        act_grad = jnp.zeros((row_count, channels), jnp.float32)
        for k in range(3):
            view = padded_grad[:, (2 - k) * spread : (2 - k) * spread + positions]
            act_grad = act_grad + jnp.dot(
                view.reshape(row_count, channels),
                conv_weight[layer_number, k].T,
                preferred_element_type=jnp.float32,
            )
        residual_float32 = stored[layer_number].astype(jnp.float32)
        pullback = jax.vjp(smooth, residual_float32)[1]
        stream_grad = stream_grad + pullback(act_grad.reshape(residual_float32.shape))[0]
    loss = loss_sum / (OUTPUT_TRACKS * weight_sum)
    return (loss, jnp.stack(kernel_grads), head_total, stream_grad.astype(jnp.bfloat16))


MESH = pl.DeviceIdType.MESH
TILE = 384
ORDERS = (("samp", 1, 2, 3), (1, "samp", 2, 3), (2, 3, "samp", 1))
CONV_CUTS = (0, 64, 128, 144)
HEAD_CUTS = (0, 16, 32, 48)
CHUNKS = LAYERS + 1
STEPS = 4
FIRST = 4 * LAYERS
LATER = FIRST + CHUNKS
LOSS = LATER + CHUNKS * len(ORDERS) * STEPS
COPIES = LOSS + STEPS + 1


def smooth_slope(values):
    scale = 0.7978845608028654
    square = values * values
    bend = jnp.tanh(scale * values * (1.0 + 0.044715 * square))
    return 0.5 * (1.0 + bend) + 0.5 * values * (1.0 - bend * bend) * scale * (
        1.0 + 3 * 0.044715 * square
    )


def dot(left, right, left_dim, right_dim):
    return lax.dot_general(
        left, right, (((left_dim,), (right_dim,)), ((), ())), preferred_element_type=jnp.float32
    )


def kernel(trunk, conv_hbm, head_hbm, targets_hbm, weights, sums, conv_out, head_out, trunk_out, *scratch):
    conv_w, head_w, counts, local_sem, send_sem, recv_sem, acts, grads, streams, slopes, stream_grad = scratch[:11]
    terms, first, later, loss_slots = (
        scratch[11 : 11 + CHUNKS],
        scratch[11 + CHUNKS : 11 + 2 * CHUNKS],
        scratch[11 + 2 * CHUNKS : -1],
        scratch[-1],
    )
    rows, channels = trunk.shape
    tracks = head_hbm.shape[1]
    seq, samp = lax.axis_index("seq"), lax.axis_index("samp")
    last = lax.axis_size("seq") - 1
    has_left, has_right = seq > 0, seq < last
    bits = [lax.rem(lax.div(seq, 2**b), 2) for b in range(4)]
    place = {"samp": samp, **{b: bits[b] for b in range(4)}}
    partner = {"samp": {"samp": 1 - samp}}
    for b in range(4):
        partner[b] = {"seq": seq + (1 - 2 * bits[b]) * 2**b}

    conv_loads = [
        pltpu.make_async_copy(conv_hbm.at[i], conv_w.at[i], local_sem.at[i]) for i in range(LAYERS)
    ]
    head_load = pltpu.make_async_copy(head_hbm, head_w, local_sem.at[LAYERS])
    count_load = pltpu.make_async_copy(targets_hbm, counts, local_sem.at[LAYERS + 1])
    for load in conv_loads + [head_load, count_load]:
        load.start()

    barrier = pltpu.get_barrier_semaphore()
    right, left = {"seq": seq + 1}, {"seq": seq - 1}
    for there in (partner["samp"], partner[1], partner[2], partner[3]):
        pl.semaphore_signal(barrier, inc=1, device_id=there, device_id_type=MESH)

    @pl.when(has_right)
    def _():
        pl.semaphore_signal(barrier, inc=1, device_id=right, device_id_type=MESH)

    @pl.when(has_left)
    def _():
        pl.semaphore_signal(barrier, inc=1, device_id=left, device_id_type=MESH)

    pl.semaphore_wait(barrier, 4 + has_right.astype(jnp.int32) + has_left.astype(jnp.int32))

    def remote(src, dst, number, there):
        return pltpu.make_async_remote_copy(
            src_ref=src,
            dst_ref=dst,
            send_sem=send_sem.at[number],
            recv_sem=recv_sem.at[number],
            device_id=there,
            device_id_type=MESH,
        )

    spreads = [BASE_DILATION * 2**i for i in range(LAYERS)]
    starts = [sum(rows + 2 * s for s in spreads[:i]) for i in range(LAYERS)]

    def edges(buffer, layer, number):
        spread, start = spreads[layer], starts[layer]
        up = remote(
            buffer.at[pl.ds(start + rows, spread)], buffer.at[pl.ds(start, spread)], number, right
        )
        down = remote(
            buffer.at[pl.ds(start + spread, spread)],
            buffer.at[pl.ds(start + spread + rows, spread)],
            number + 1,
            left,
        )
        return up, down

    def send_edges(buffer, layer, number, block):
        spread, start = spreads[layer], starts[layer]
        buffer[pl.ds(start + spread, rows)] = block
        up, down = edges(buffer, layer, number)

        @pl.when(has_right)
        def _():
            up.start()

        @pl.when(has_left)
        def _():
            down.start()

        @pl.when(jnp.logical_not(has_left))
        def _():
            buffer[pl.ds(start, spread)] = jnp.zeros((spread, channels), jnp.bfloat16)

        @pl.when(jnp.logical_not(has_right))
        def _():
            buffer[pl.ds(start + spread + rows, spread)] = jnp.zeros((spread, channels), jnp.bfloat16)

    def wait_edges(buffer, layer, number):
        up, down = edges(buffer, layer, number)

        @pl.when(has_right)
        def _():
            up.wait_send()
            down.wait_recv()

        @pl.when(has_left)
        def _():
            down.wait_send()
            up.wait_recv()

    def view(buffer, layer, tap):
        return buffer[pl.ds(starts[layer] + tap * spreads[layer], rows)]

    streams[0] = trunk[...]
    for layer in range(LAYERS):
        send_edges(
            acts, layer, 2 * layer, smooth(streams[layer].astype(jnp.float32)).astype(jnp.bfloat16)
        )
        conv_loads[layer].wait()
        total = streams[layer].astype(jnp.float32) + dot(view(acts, layer, 1), conv_w[layer, 1], 1, 0)
        wait_edges(acts, layer, 2 * layer)
        for tap in (0, 2):
            total += dot(view(acts, layer, tap), conv_w[layer, tap], 1, 0)
        streams[layer + 1] = total.astype(jnp.bfloat16)

    head_load.wait()
    count_load.wait()
    stream_grad[...] = jnp.zeros_like(stream_grad)

    def folded(values):
        return jnp.sum(values.reshape(rows // 8, 8, values.shape[1]), axis=0)

    sums[0:8] = jnp.zeros((8, 128), jnp.float32)
    sums[8:16] = folded(weights[...])

    def head_tile(step, carry):
        place_of = pl.ds(pl.multiple_of(step * TILE, 128), TILE)
        matrix = head_w[:, place_of]
        logits = dot(streams[LAYERS], matrix, 1, 0)
        weight = jnp.concatenate([weights[...]] * (TILE // 128), axis=1)
        tail = jnp.exp(-jnp.abs(logits))
        predicted = jnp.maximum(logits, 0.0) + jnp.log1p(tail)
        slope = jnp.where(logits >= 0, 1.0, tail) / (1.0 + tail)
        seen = counts[:, place_of].astype(jnp.float32)
        fold = folded(weight * (predicted - seen * jnp.log(predicted)))
        sums[0:8] += sum(fold[:, i * 128 : (i + 1) * 128] for i in range(TILE // 128))
        grad = (weight * (1.0 - seen / predicted) * slope).astype(jnp.bfloat16)
        slopes[:, place_of] = grad
        stream_grad[...] += dot(grad, matrix, 1, 1)
        return carry

    lax.fori_loop(0, tracks // TILE, head_tile, 0)

    def first_copy(chunk):
        return remote(
            terms[chunk].at[:, :, :, :, 1 - bits[0]], first[chunk], FIRST + chunk, partner[0]
        )

    def part_rows(chunk, part):
        cuts = HEAD_CUTS if chunk == 0 else CONV_CUTS
        return pl.ds(cuts[part], cuts[part + 1] - cuts[part])

    def slot(chunk, part, step):
        return later[(chunk * len(ORDERS) + part) * STEPS + step]

    def picked(chunk, part, step, which):
        order = ORDERS[part]
        labels = ["samp", 3, 2, 1]
        for done in order[:step]:
            labels.remove(done)
        dim = labels.index(order[step])
        index = place[order[step]] if which == 0 else 1 - place[order[step]]
        return labels, dim, index

    def later_copy(chunk, part, step):
        labels, dim, index = picked(chunk, part, step, 1)
        at = [slice(None)] * len(labels)
        at[dim] = index
        if step == 0:
            src = first[chunk].at[tuple(at) + (part_rows(chunk, part),)]
        else:
            src = slot(chunk, part, step - 1).at[tuple(at)]
        number = LATER + (chunk * len(ORDERS) + part) * STEPS + step
        return remote(src, slot(chunk, part, step), number, partner[ORDERS[part][step]])

    def added(a, b):
        return a.astype(jnp.float32) + b.astype(jnp.float32)

    def digits(number, count):
        return tuple(lax.rem(lax.div(number, 2 ** (count - 1 - i)), 2) for i in range(count))

    def start_later(chunk):
        first_copy(chunk).wait()

        def add(number, carry):
            at = digits(number, 4)
            first[chunk][at] = added(first[chunk][at], terms[chunk][at + (bits[0],)]).astype(
                jnp.bfloat16
            )
            return carry

        lax.fori_loop(0, 16, add, 0)
        for part in range(len(ORDERS)):
            later_copy(chunk, part, 0).start()

    def advance(chunk, step):
        for part in range(len(ORDERS)):
            later_copy(chunk, part, step).wait()
            labels, dim, index = picked(chunk, part, step, 0)
            held = slot(chunk, part, step)
            before = first[chunk] if step == 0 else slot(chunk, part, step - 1)
            count = len(labels) - 1

            def values(at):
                there = at[:dim] + (index,) + at[dim:]
                if step == 0:
                    there = there + (part_rows(chunk, part),)
                return added(held[at] if at else held[...], before[there])

            if step == STEPS - 1:
                where = part_rows(chunk, part)
                if chunk == 0:
                    head_out[where] = values(())
                else:
                    conv_out[chunk - 1, where] = values(())
            else:

                def add(number, carry):
                    at = digits(number, count)
                    held[at] = values(at).astype(jnp.bfloat16)
                    return carry

                lax.fori_loop(0, 2**count, add, 0)
                later_copy(chunk, part, step + 1).start()

    def loss_copy(step):
        there = partner[(0, "samp", 1, 2, 3)[step]]
        return remote(loss_slots.at[2 * step], loss_slots.at[2 * step + 1], LOSS + step, there)

    def loss_start(step):
        loss_slots[2 * step] = sums[...]
        loss_copy(step).start()

    def loss_end(step):
        loss_copy(step).wait()
        sums[...] += loss_slots[2 * step + 1]

    def put(chunk, value, row, side):
        size = terms[chunk].shape[5]
        at = 0
        while at < value.shape[0]:
            block, inner = divmod(row + at, size)
            length = min(size - inner, value.shape[0] - at)
            where = (side,) + tuple((block >> b) & 1 for b in (3, 2, 1, 0))
            terms[chunk][where + (pl.ds(inner, length),)] = value[at : at + length].astype(jnp.bfloat16)
            at += length

    loss_start(0)
    wide = head_out.shape[1]
    for side in range(2):
        base = side * (tracks - wide)
        for begin in range(0, wide, 512):
            width = min(512, wide - begin)
            value = dot(streams[LAYERS], slopes[:, base + begin : base + begin + width], 0, 0)
            for block in range(16):
                where = (side,) + tuple((block >> b) & 1 for b in (3, 2, 1, 0))
                terms[0][where + (slice(None), pl.ds(begin, width))] = value[
                    block * 48 : (block + 1) * 48
                ].astype(jnp.bfloat16)
    first_copy(0).start()

    chunk = 0
    for layer in reversed(range(LAYERS)):
        number = 2 * LAYERS + 2 * layer
        send_edges(grads, layer, number, stream_grad[...].astype(jnp.bfloat16))
        middle = view(grads, layer, 1)
        for tap in range(3):
            for begin in range(0, channels, 384):
                seen = acts[pl.ds(starts[layer] + tap * spreads[layer], rows), begin : begin + 384]
                value = dot(seen, middle, 0, 0)
                for side in range(2):
                    put(
                        layer + 1,
                        value[:, side * channels // 2 : (side + 1) * channels // 2],
                        tap * channels + begin,
                        side,
                    )
        first_copy(layer + 1).start()
        start_later(chunk)
        chunk = layer + 1
        loss_end(LAYERS - 1 - layer)
        loss_start(LAYERS - layer)
        total = dot(middle, conv_w[layer, 1], 1, 1)
        wait_edges(grads, layer, number)
        for tap in (0, 2):
            total += dot(view(grads, layer, 2 - tap), conv_w[layer, tap], 1, 1)
        stream_grad[...] += smooth_slope(streams[layer].astype(jnp.float32)) * total
    start_later(1)
    trunk_out[...] = stream_grad[...]
    loss_end(3)
    loss_start(4)
    turns = ((0, 0), (3, 0), (0, 1), (2, 0), (3, 1), (0, 2), (1, 0), (2, 1), (3, 2), (0, 3), (1, 1), (2, 2), (3, 3), (1, 2), (2, 3), (1, 3))
    for chunk, step in turns:
        advance(chunk, step)
    loss_end(4)


def per_device_kernel(trunk, conv_weight, head_weight, targets, error_mask, upweight):
    windows, rows, channels = trunk.shape
    devices = lax.axis_size("seq")
    tracks = head_weight.shape[1]
    bins_all = windows * rows * devices * lax.axis_size("samp")
    bin_weight = jnp.where(error_mask == 1, upweight, 1).astype(jnp.float32)
    spreads = [BASE_DILATION * 2**i for i in range(LAYERS)]
    extended_rows = sum(rows + 2 * s for s in spreads)
    half = tracks // 2
    wide = (half + 127) // 128 * 128
    sizes = [(channels // devices, wide)] + [(3 * channels // devices, channels // 2)] * LAYERS
    cuts = [HEAD_CUTS] + [CONV_CUTS] * LAYERS
    vmem = functools.partial(pltpu.VMEM, dtype=jnp.bfloat16)
    scratch = [
        vmem(conv_weight.shape),
        vmem(head_weight.shape),
        pltpu.VMEM((rows, tracks), jnp.int32),
        pltpu.SemaphoreType.DMA((LAYERS + 2,)),
        pltpu.SemaphoreType.DMA((COPIES,)),
        pltpu.SemaphoreType.DMA((COPIES,)),
        vmem((extended_rows, channels)),
        vmem((extended_rows, channels)),
        vmem((LAYERS + 1, rows, channels)),
        vmem((rows, tracks)),
        pltpu.VMEM((rows, channels), jnp.float32),
    ]
    scratch += [vmem((2,) * 5 + size) for size in sizes]
    scratch += [vmem((2,) * 4 + size) for size in sizes]
    for size, cut in zip(sizes, cuts):
        for part in range(len(ORDERS)):
            for step in range(STEPS):
                scratch.append(vmem((2,) * (3 - step) + (cut[part + 1] - cut[part], size[1])))
    scratch.append(pltpu.VMEM((2 * (STEPS + 1), 16, 128), jnp.float32))
    whole = pl.BlockSpec(memory_space=pltpu.VMEM)
    away = pl.BlockSpec(memory_space=pl.ANY)
    sums, conv_grad, head_grad, trunk_grad = pl.pallas_call(
        kernel,
        out_shape=(
            jax.ShapeDtypeStruct((16, 128), jnp.float32),
            jax.ShapeDtypeStruct((LAYERS,) + sizes[1], jnp.float32),
            jax.ShapeDtypeStruct(sizes[0], jnp.float32),
            jax.ShapeDtypeStruct((rows, channels), jnp.float32),
        ),
        in_specs=[whole, away, away, away, whole],
        out_specs=(whole,) * 4,
        scratch_shapes=scratch,
        compiler_params=pltpu.CompilerParams(
            collective_id=0, has_side_effects=True, vmem_limit_bytes=63 * 2**20
        ),
    )(
        trunk.reshape(rows, channels),
        conv_weight,
        head_weight,
        targets.reshape(rows, tracks),
        jnp.broadcast_to(bin_weight.reshape(rows, 1), (rows, 128)),
    )
    weight_sum = jnp.sum(sums[8:16, 0])
    loss = jnp.sum(sums[0:8]) / (OUTPUT_TRACKS * weight_sum)
    factor = bins_all / weight_sum
    head_grad = lax.dynamic_slice_in_dim(
        head_grad, lax.axis_index("samp") * (wide - half), half, axis=1
    )
    return (
        loss,
        conv_grad * factor,
        head_grad * factor,
        (trunk_grad * factor).astype(jnp.bfloat16).reshape(trunk.shape),
    )


def fits(mesh):
    return mesh.shape["seq"] == 16 and mesh.shape["samp"] == 2


def solution(mesh):
    return jax.shard_map(
        per_device_kernel if fits(mesh) else per_device,
        mesh=mesh,
        in_specs=(
            P("samp", "seq", None),
            P(),
            P(),
            P("samp", "seq", None),
            P("samp", "seq"),
            P("samp", "seq"),
        ),
        out_specs=(P(), P(None, "seq", "samp"), P("seq", "samp"), P("samp", "seq", None)),
        check_vma=False,
    )
```

```python
import functools

import jax
import jax.numpy as jnp
from jax import lax
from jax.experimental import pallas as pl
from jax.experimental.pallas import tpu as pltpu
from jax.sharding import PartitionSpec as P

OUTPUT_TRACKS = 2688
LAYERS = 3
BASE_DILATION = 64


def extended(shard, width):
    devices, length = (lax.axis_size("seq"), shard.shape[1])
    up = [(i, (i + 1) % devices) for i in range(devices - 1)]
    down = [(j, i) for i, j in up]
    before = lax.ppermute(lax.slice_in_dim(shard, length - width, length, axis=1), "seq", up)
    after = lax.ppermute(lax.slice_in_dim(shard, 0, width, axis=1), "seq", down)
    return jnp.concatenate([before, shard, after], axis=1)


def smooth(values):
    return jax.nn.gelu(values, approximate=True)


def halve(part, dim, axis, bit):
    place = lax.axis_index(axis)
    mine = lax.rem(lax.div(place, 2**bit), 2)
    pairs = [(i, i ^ (2**bit)) for i in range(lax.axis_size(axis))]
    away = lax.dynamic_index_in_dim(part, 1 - mine, dim, keepdims=False)
    kept = lax.dynamic_index_in_dim(part, mine, dim, keepdims=False)
    come = lax.ppermute(away, axis, pairs)
    return (kept.astype(jnp.float32) + come.astype(jnp.float32)).astype(jnp.bfloat16)


def scatter_sum(part, order):
    labels = ["samp"] + list(reversed(range(part.ndim - 3)))
    for step in order:
        dim = labels.index(step)
        part = halve(part, dim, *(("samp", 0) if step == "samp" else ("seq", step)))
        labels.pop(dim)
    return part


def reduced(halves):
    devices = lax.axis_size("seq")
    bits = devices.bit_length() - 1
    rows = halves[0].shape[0] // devices
    stacked = jnp.stack([h.reshape((2,) * bits + (rows, h.shape[1])) for h in halves], axis=0)
    cut = max((rows * 5 // 9) // 16 * 16, 1)
    higher = list(range(2, bits))
    first = scatter_sum(stacked[..., :cut, :], [0, "samp", 1] + higher)
    second = scatter_sum(stacked[..., cut:, :], [0, 1, "samp"] + higher)
    return jnp.concatenate([first, second], axis=0).astype(jnp.float32)


def per_device(trunk, conv_weight, head_weight, targets, error_mask, upweight):
    windows, positions, channels = trunk.shape
    row_count = windows * positions
    bins_all = row_count * lax.axis_size("seq") * lax.axis_size("samp")
    bin_weight = jnp.where(error_mask == 1, upweight, 1).astype(jnp.float32)
    weight_sum = lax.psum(jnp.sum(bin_weight), ("seq", "samp"))
    stream = trunk
    stored = []
    padded_acts = []
    for layer_number in range(LAYERS):
        spread = BASE_DILATION * 2**layer_number
        activated = smooth(stream.astype(jnp.float32)).astype(jnp.bfloat16)
        padded = extended(activated, spread)
        taps = jnp.concatenate(
            [padded[:, k * spread : k * spread + positions] for k in range(3)], axis=2
        ).reshape(row_count, 3 * channels)
        conv_out = jnp.dot(
            taps,
            conv_weight[layer_number].reshape(3 * channels, channels),
            preferred_element_type=jnp.float32,
        )
        stored.append(stream)
        padded_acts.append(taps)
        stream = (stream.astype(jnp.float32) + conv_out.reshape(stream.shape)).astype(jnp.bfloat16)
    residual_rows = stream.reshape(row_count, channels)
    logits = jnp.dot(residual_rows, head_weight, preferred_element_type=jnp.float32)
    predicted = jax.nn.softplus(logits)
    slope = jax.nn.sigmoid(logits)
    counts = targets.reshape(row_count, -1).astype(jnp.float32)
    flat_weight = bin_weight.reshape(row_count, 1)
    partial_loss = jnp.sum(flat_weight * (predicted - counts * jnp.log(predicted)))
    loss_sum = lax.psum(partial_loss, ("seq", "samp"))
    factor = bins_all / weight_sum
    logit_grad = (factor * flat_weight * (1.0 - counts / predicted) * slope).astype(jnp.bfloat16)
    half = logit_grad.shape[1] // 2
    head_total = reduced(
        [
            jnp.dot(residual_rows.T, part, preferred_element_type=jnp.float32).astype(jnp.bfloat16)
            for part in (logit_grad[:, :half], logit_grad[:, half:])
        ]
    )
    stream_grad = jnp.dot(logit_grad, head_weight.T, preferred_element_type=jnp.float32).reshape(
        windows, positions, channels
    )
    kernel_grads = [None] * LAYERS
    for layer_number in reversed(range(LAYERS)):
        spread = BASE_DILATION * 2**layer_number
        grad_bf = stream_grad.astype(jnp.bfloat16)
        grad_flat = grad_bf.reshape(row_count, channels)
        padded_grad = extended(grad_bf, spread)
        side = channels // 2
        kernel_grads[layer_number] = reduced(
            [
                jnp.dot(
                    padded_acts[layer_number].T, part, preferred_element_type=jnp.float32
                ).astype(jnp.bfloat16)
                for part in (grad_flat[:, :side], grad_flat[:, side:])
            ]
        )
        act_grad = jnp.zeros((row_count, channels), jnp.float32)
        for k in range(3):
            view = padded_grad[:, (2 - k) * spread : (2 - k) * spread + positions]
            act_grad = act_grad + jnp.dot(
                view.reshape(row_count, channels),
                conv_weight[layer_number, k].T,
                preferred_element_type=jnp.float32,
            )
        residual_float32 = stored[layer_number].astype(jnp.float32)
        pullback = jax.vjp(smooth, residual_float32)[1]
        stream_grad = stream_grad + pullback(act_grad.reshape(residual_float32.shape))[0]
    loss = loss_sum / (OUTPUT_TRACKS * weight_sum)
    return (loss, jnp.stack(kernel_grads), head_total, stream_grad.astype(jnp.bfloat16))


MESH = pl.DeviceIdType.MESH
TILE = 384
ORDERS = (("samp", 1, 2, 3), (1, "samp", 2, 3), (2, 3, "samp", 1))
CUTS = ((0, 16, 32, 48), (0, 48, 96, 144), (0, 64, 128, 144), (0, 64, 128, 144))
CHUNKS = LAYERS + 1
TURNS = {
    0: (),
    3: ((0, 0, 0), (0, 1, 0), (0, 2, 0), (3, 2, 0)),
    2: ((3, 0, 0), (3, 1, 0), (2, 2, 0)),
    1: (
        (0, 2, 1), (3, 2, 1), (2, 0, 0), (2, 1, 0), (0, 0, 1), (0, 1, 1), (1, 2, 0), (2, 2, 1),
        (0, 0, 2), (0, 1, 2), (1, 0, 0), (1, 1, 0), (1, 2, 1), (0, 0, 3), (3, 0, 1), (3, 1, 1),
        (0, 1, 3), (0, 2, 2), (3, 2, 2), (3, 0, 2), (2, 0, 1), (3, 1, 2), (2, 1, 1), (3, 0, 3),
        (2, 2, 2), (1, 0, 1), (0, 2, 3), (3, 2, 3), (2, 0, 2), (2, 2, 3), (3, 1, 3), (1, 1, 1),
        (1, 2, 2), (2, 1, 2), (1, 0, 2), (1, 2, 3), (2, 0, 3), (1, 1, 2), (2, 1, 3), (1, 0, 3),
        (1, 1, 3),
    ),
}
STEPS = 4
FIRST = 4 * LAYERS
LATER = FIRST + CHUNKS
LOSS = LATER + CHUNKS * len(ORDERS) * STEPS
COPIES = LOSS + STEPS + 1


def smooth_slope(values):
    scale = 0.7978845608028654
    square = values * values
    bend = jnp.tanh(scale * values * (1.0 + 0.044715 * square))
    return 0.5 * (1.0 + bend) + 0.5 * values * (1.0 - bend * bend) * scale * (
        1.0 + 3 * 0.044715 * square
    )


def dot(left, right, left_dim, right_dim):
    return lax.dot_general(
        left, right, (((left_dim,), (right_dim,)), ((), ())), preferred_element_type=jnp.float32
    )


def kernel(
    trunk, conv_hbm, head_hbm, targets_hbm, mask, upweight, loss_out, conv_out, head_out, trunk_out, *scratch
):
    conv_w, head_w, counts, local_sem, send_sem, recv_sem, acts, grads, streams, slopes = scratch[:10]
    stream_grad, weights, sums, turned = scratch[10:14]
    scratch = scratch[3:]
    terms, first, later, loss_slots = (
        scratch[11 : 11 + CHUNKS],
        scratch[11 + CHUNKS : 11 + 2 * CHUNKS],
        scratch[11 + 2 * CHUNKS : -1],
        scratch[-1],
    )
    rows, channels = trunk.shape
    tracks = head_hbm.shape[1]
    seq, samp = lax.axis_index("seq"), lax.axis_index("samp")
    last = lax.axis_size("seq") - 1
    has_left, has_right = seq > 0, seq < last
    bits = [lax.rem(lax.div(seq, 2**b), 2) for b in range(4)]
    place = {"samp": samp, **{b: bits[b] for b in range(4)}}
    partner = {"samp": {"samp": 1 - samp}}
    for b in range(4):
        partner[b] = {"seq": seq + (1 - 2 * bits[b]) * 2**b}

    conv_loads = [
        pltpu.make_async_copy(conv_hbm.at[i], conv_w.at[i], local_sem.at[i]) for i in range(LAYERS)
    ]
    head_load = pltpu.make_async_copy(head_hbm, head_w, local_sem.at[LAYERS])
    count_load = pltpu.make_async_copy(targets_hbm, counts, local_sem.at[LAYERS + 1])
    for load in conv_loads + [head_load, count_load]:
        load.start()

    streams[0] = trunk[...]
    first_act = smooth(trunk[...].astype(jnp.float32)).astype(jnp.bfloat16)
    row = jnp.where(mask[...] == 1, upweight[...], 1).astype(jnp.float32)
    weights[...] = jnp.broadcast_to(row, (128, rows)).T

    barrier = pltpu.get_barrier_semaphore()
    right, left = {"seq": seq + 1}, {"seq": seq - 1}
    for there in (partner["samp"], partner[1], partner[2], partner[3]):
        pl.semaphore_signal(barrier, inc=1, device_id=there, device_id_type=MESH)

    @pl.when(has_right)
    def _():
        pl.semaphore_signal(barrier, inc=1, device_id=right, device_id_type=MESH)

    @pl.when(has_left)
    def _():
        pl.semaphore_signal(barrier, inc=1, device_id=left, device_id_type=MESH)

    pl.semaphore_wait(barrier, 4 + has_right.astype(jnp.int32) + has_left.astype(jnp.int32))

    def remote(src, dst, number, there):
        return pltpu.make_async_remote_copy(
            src_ref=src,
            dst_ref=dst,
            send_sem=send_sem.at[number],
            recv_sem=recv_sem.at[number],
            device_id=there,
            device_id_type=MESH,
        )

    spreads = [BASE_DILATION * 2**i for i in range(LAYERS)]
    starts = [sum(rows + 2 * s for s in spreads[:i]) for i in range(LAYERS)]

    def edges(buffer, layer, number):
        spread, start = spreads[layer], starts[layer]
        up = remote(
            buffer.at[pl.ds(start + rows, spread)], buffer.at[pl.ds(start, spread)], number, right
        )
        down = remote(
            buffer.at[pl.ds(start + spread, spread)],
            buffer.at[pl.ds(start + spread + rows, spread)],
            number + 1,
            left,
        )
        return up, down

    def send_edges(buffer, layer, number, block):
        spread, start = spreads[layer], starts[layer]
        buffer[pl.ds(start + spread, rows)] = block
        up, down = edges(buffer, layer, number)

        @pl.when(has_right)
        def _():
            up.start()

        @pl.when(has_left)
        def _():
            down.start()

        @pl.when(jnp.logical_not(has_left))
        def _():
            buffer[pl.ds(start, spread)] = jnp.zeros((spread, channels), jnp.bfloat16)

        @pl.when(jnp.logical_not(has_right))
        def _():
            buffer[pl.ds(start + spread + rows, spread)] = jnp.zeros((spread, channels), jnp.bfloat16)

    def wait_edges(buffer, layer, number):
        up, down = edges(buffer, layer, number)

        @pl.when(has_right)
        def _():
            up.wait_send()
            down.wait_recv()

        @pl.when(has_left)
        def _():
            down.wait_send()
            up.wait_recv()

    def view(buffer, layer, tap):
        return buffer[pl.ds(starts[layer] + tap * spreads[layer], rows)]

    for layer in range(LAYERS):
        block = first_act
        if layer > 0:
            block = smooth(streams[layer].astype(jnp.float32)).astype(jnp.bfloat16)
        send_edges(acts, layer, 2 * layer, block)
        conv_loads[layer].wait()
        total = streams[layer].astype(jnp.float32) + dot(view(acts, layer, 1), conv_w[layer, 1], 1, 0)
        wait_edges(acts, layer, 2 * layer)
        for tap in (0, 2):
            total += dot(view(acts, layer, tap), conv_w[layer, tap], 1, 0)
        streams[layer + 1] = total.astype(jnp.bfloat16)

    head_load.wait()
    count_load.wait()
    turned[...] = streams[LAYERS][...].T

    def folded(values):
        return jnp.sum(values.reshape(rows // 8, 8, values.shape[1]), axis=0)

    def first_copy(chunk):
        return remote(
            terms[chunk].at[:, :, :, :, 1 - bits[0]], first[chunk], FIRST + chunk, partner[0]
        )

    def part_rows(chunk, part):
        return pl.ds(CUTS[chunk][part], CUTS[chunk][part + 1] - CUTS[chunk][part])

    def slot(chunk, part, step):
        return later[(chunk * len(ORDERS) + part) * STEPS + step]

    def picked(chunk, part, step, which):
        order = ORDERS[part]
        labels = ["samp", 3, 2, 1]
        for done in order[:step]:
            labels.remove(done)
        dim = labels.index(order[step])
        index = place[order[step]] if which == 0 else 1 - place[order[step]]
        return labels, dim, index

    def later_copy(chunk, part, step):
        labels, dim, index = picked(chunk, part, step, 1)
        at = [slice(None)] * len(labels)
        at[dim] = index
        if step == 0:
            src = first[chunk].at[tuple(at) + (part_rows(chunk, part),)]
        else:
            src = slot(chunk, part, step - 1).at[tuple(at)]
        number = LATER + (chunk * len(ORDERS) + part) * STEPS + step
        return remote(src, slot(chunk, part, step), number, partner[ORDERS[part][step]])

    def added(a, b):
        return a.astype(jnp.float32) + b.astype(jnp.float32)

    def digits(number, count):
        return tuple(lax.rem(lax.div(number, 2 ** (count - 1 - i)), 2) for i in range(count))

    def start_later(chunk):
        first_copy(chunk).wait()

        def add(number, carry):
            at = digits(number, 4)
            first[chunk][at] = added(first[chunk][at], terms[chunk][at + (bits[0],)]).astype(
                jnp.bfloat16
            )
            return carry

        lax.fori_loop(0, 16, add, 0)
        for part in range(len(ORDERS)):
            later_copy(chunk, part, 0).start()

    def advance(chunk, part, step):
        later_copy(chunk, part, step).wait()
        labels, dim, index = picked(chunk, part, step, 0)
        held = slot(chunk, part, step)
        before = first[chunk] if step == 0 else slot(chunk, part, step - 1)
        count = len(labels) - 1

        def values(at):
            there = at[:dim] + (index,) + at[dim:]
            if step == 0:
                there = there + (part_rows(chunk, part),)
            return added(held[at] if at else held[...], before[there])

        if step == STEPS - 1:
            where = part_rows(chunk, part)
            total = values(()) * factor()
            if chunk == 0:
                half = head_out.shape[1]
                moved = pltpu.roll(total, half, axis=1)
                head_out[where] = jnp.where(samp == 1, moved, total)[:, :half]
            else:
                conv_out[chunk - 1, where] = total
        else:

            def add(number, carry):
                at = digits(number, count)
                held[at] = values(at).astype(jnp.bfloat16)
                return carry

            lax.fori_loop(0, 2**count, add, 0)
            later_copy(chunk, part, step + 1).start()

    def weight_sum():
        return jnp.sum(sums[8:16, 0:1], axis=0, keepdims=True)

    def factor():
        bins_all = float(rows) * lax.axis_size("seq") * lax.axis_size("samp")
        return bins_all / weight_sum()

    def loss_copy(step):
        there = partner[(0, "samp", 1, 2, 3)[step]]
        return remote(loss_slots.at[2 * step], loss_slots.at[2 * step + 1], LOSS + step, there)

    def loss_start(step):
        loss_slots[2 * step] = sums[...]
        loss_copy(step).start()

    def loss_end(step):
        loss_copy(step).wait()
        sums[...] += loss_slots[2 * step + 1]

    def put(chunk, value, row, side):
        size = terms[chunk].shape[5]
        at = 0
        while at < value.shape[0]:
            block, inner = divmod(row + at, size)
            length = min(size - inner, value.shape[0] - at)
            where = (side,) + tuple((block >> b) & 1 for b in (3, 2, 1, 0))
            terms[chunk][where + (pl.ds(inner, length),)] = value[at : at + length].astype(jnp.bfloat16)
            at += length

    wide = terms[0].shape[6]
    loss_fold = jnp.zeros((8, 128), jnp.float32)
    for tile in range(tracks // TILE):
        begin = tile * TILE
        matrix = head_w[:, begin : begin + TILE]
        logits = dot(streams[LAYERS], matrix, 1, 0)
        weight = jnp.concatenate([weights[...]] * (TILE // 128), axis=1)
        tail = jnp.exp(-jnp.abs(logits))
        above = 1.0 + tail
        inverse = 1.0 / above
        predicted = jnp.maximum(logits, 0.0) + (jnp.log(above) + (tail - (above - 1.0)) * inverse)
        slope = jnp.where(logits >= 0, 1.0, tail) * inverse
        seen = counts[:, begin : begin + TILE].astype(jnp.float32)
        fold = folded(weight * (predicted - seen * jnp.log(predicted)))
        loss_fold += sum(fold[:, i * 128 : (i + 1) * 128] for i in range(TILE // 128))
        grad = (weight * (1.0 - seen / predicted) * slope).astype(jnp.bfloat16)
        slopes[:, begin : begin + TILE] = grad
        value = dot(turned[...], grad, 1, 0).astype(jnp.bfloat16)
        for side in range(2):
            base = side * (tracks - wide)
            low, high = max(begin, base), min(begin + TILE, base + wide)
            if low < high:
                for block in range(16):
                    where = (side,) + tuple((block >> b) & 1 for b in (3, 2, 1, 0))
                    terms[0][where + (slice(None), pl.ds(low - base, high - low))] = value[
                        block * 48 : (block + 1) * 48, low - begin : high - begin
                    ]
    first_copy(0).start()
    sums[0:8] = loss_fold
    sums[8:16] = folded(weights[...])
    loss_start(0)
    stream_grad[...] = dot(slopes[...], head_w[...], 1, 1)

    def begin_and_turn(chunk):
        start_later(chunk)
        for turn in TURNS[chunk]:
            advance(*turn)

    chunk = 0
    for layer in reversed(range(LAYERS)):
        number = 2 * LAYERS + 2 * layer
        send_edges(grads, layer, number, stream_grad[...].astype(jnp.bfloat16))
        middle = view(grads, layer, 1)
        for tap in range(3):
            for begin in range(0, channels, 384):
                seen = acts[pl.ds(starts[layer] + tap * spreads[layer], rows), begin : begin + 384]
                value = dot(seen, middle, 0, 0)
                for side in range(2):
                    put(
                        layer + 1,
                        value[:, side * channels // 2 : (side + 1) * channels // 2],
                        tap * channels + begin,
                        side,
                    )
        first_copy(layer + 1).start()
        begin_and_turn(chunk)
        chunk = layer + 1
        loss_end(LAYERS - 1 - layer)
        loss_start(LAYERS - layer)
        total = dot(middle, conv_w[layer, 1], 1, 1)
        wait_edges(grads, layer, number)
        for tap in (0, 2):
            total += dot(view(grads, layer, 2 - tap), conv_w[layer, tap], 1, 1)
        stream_grad[...] += smooth_slope(streams[layer].astype(jnp.float32)) * total
    loss_end(3)
    loss_start(4)
    start_later(1)
    loss_end(4)
    trunk_out[...] = (stream_grad[...] * factor()).astype(jnp.bfloat16)
    loss_out[...] = jnp.sum(
        jnp.sum(sums[0:8], axis=0, keepdims=True), axis=1, keepdims=True
    ) / (OUTPUT_TRACKS * weight_sum())
    for turn in TURNS[1]:
        advance(*turn)


def per_device_kernel(trunk, conv_weight, head_weight, targets, error_mask, upweight):
    windows, rows, channels = trunk.shape
    devices = lax.axis_size("seq")
    tracks = head_weight.shape[1]
    spreads = [BASE_DILATION * 2**i for i in range(LAYERS)]
    extended_rows = sum(rows + 2 * s for s in spreads)
    half = tracks // 2
    wide = (half + 127) // 128 * 128
    sizes = [(channels // devices, wide)] + [(3 * channels // devices, channels // 2)] * LAYERS
    vmem = functools.partial(pltpu.VMEM, dtype=jnp.bfloat16)
    scratch = [
        vmem(conv_weight.shape),
        vmem(head_weight.shape),
        pltpu.VMEM((rows, tracks), jnp.int32),
        pltpu.SemaphoreType.DMA((LAYERS + 2,)),
        pltpu.SemaphoreType.DMA((COPIES,)),
        pltpu.SemaphoreType.DMA((COPIES,)),
        vmem((extended_rows, channels)),
        vmem((extended_rows, channels)),
        vmem((LAYERS + 1, rows, channels)),
        vmem((rows, tracks)),
        pltpu.VMEM((rows, channels), jnp.float32),
        pltpu.VMEM((rows, 128), jnp.float32),
        pltpu.VMEM((16, 128), jnp.float32),
        vmem((channels, rows)),
    ]
    scratch += [vmem((2,) * 5 + size) for size in sizes]
    scratch += [vmem((2,) * 4 + size) for size in sizes]
    for size, cut in zip(sizes, CUTS):
        for part in range(len(ORDERS)):
            for step in range(STEPS):
                scratch.append(vmem((2,) * (3 - step) + (cut[part + 1] - cut[part], size[1])))
    scratch.append(pltpu.VMEM((2 * (STEPS + 1), 16, 128), jnp.float32))
    whole = pl.BlockSpec(memory_space=pltpu.VMEM)
    away = pl.BlockSpec(memory_space=pl.ANY)
    loss, conv_grad, head_grad, trunk_grad = pl.pallas_call(
        kernel,
        out_shape=(
            jax.ShapeDtypeStruct((1, 1), jnp.float32),
            jax.ShapeDtypeStruct((LAYERS,) + sizes[1], jnp.float32),
            jax.ShapeDtypeStruct((sizes[0][0], half), jnp.float32),
            jax.ShapeDtypeStruct((rows, channels), jnp.bfloat16),
        ),
        in_specs=[whole, away, away, away, whole, whole],
        out_specs=(whole,) * 4,
        scratch_shapes=scratch,
        compiler_params=pltpu.CompilerParams(
            collective_id=0, has_side_effects=True, vmem_limit_bytes=63 * 2**20
        ),
    )(
        trunk.reshape(rows, channels),
        conv_weight,
        head_weight,
        targets.reshape(rows, tracks),
        error_mask,
        upweight,
    )
    return loss.reshape(()), conv_grad, head_grad, trunk_grad.reshape(trunk.shape)


def fits(mesh):
    return mesh.shape["seq"] == 16 and mesh.shape["samp"] == 2


def solution(mesh):
    return jax.shard_map(
        per_device_kernel if fits(mesh) else per_device,
        mesh=mesh,
        in_specs=(
            P("samp", "seq", None),
            P(),
            P(),
            P("samp", "seq", None),
            P("samp", "seq"),
            P("samp", "seq"),
        ),
        out_specs=(P(), P(None, "seq", "samp"), P("seq", "samp"), P("samp", "seq", None)),
        check_vma=False,
    )
```

```python
import functools

import jax
import jax.numpy as jnp
from jax import lax
from jax.experimental import pallas as pl
from jax.experimental.pallas import tpu as pltpu
from jax.sharding import PartitionSpec as P

OUTPUT_TRACKS = 2688
LAYERS = 3
BASE_DILATION = 64


def extended(shard, width):
    devices, length = (lax.axis_size("seq"), shard.shape[1])
    up = [(i, (i + 1) % devices) for i in range(devices - 1)]
    down = [(j, i) for i, j in up]
    before = lax.ppermute(lax.slice_in_dim(shard, length - width, length, axis=1), "seq", up)
    after = lax.ppermute(lax.slice_in_dim(shard, 0, width, axis=1), "seq", down)
    return jnp.concatenate([before, shard, after], axis=1)


def smooth(values):
    return jax.nn.gelu(values, approximate=True)


def halve(part, dim, axis, bit):
    place = lax.axis_index(axis)
    mine = lax.rem(lax.div(place, 2**bit), 2)
    pairs = [(i, i ^ (2**bit)) for i in range(lax.axis_size(axis))]
    away = lax.dynamic_index_in_dim(part, 1 - mine, dim, keepdims=False)
    kept = lax.dynamic_index_in_dim(part, mine, dim, keepdims=False)
    come = lax.ppermute(away, axis, pairs)
    return (kept.astype(jnp.float32) + come.astype(jnp.float32)).astype(jnp.bfloat16)


def scatter_sum(part, order):
    labels = ["samp"] + list(reversed(range(part.ndim - 3)))
    for step in order:
        dim = labels.index(step)
        part = halve(part, dim, *(("samp", 0) if step == "samp" else ("seq", step)))
        labels.pop(dim)
    return part


def reduced(halves):
    devices = lax.axis_size("seq")
    bits = devices.bit_length() - 1
    rows = halves[0].shape[0] // devices
    stacked = jnp.stack([h.reshape((2,) * bits + (rows, h.shape[1])) for h in halves], axis=0)
    cut = max((rows * 5 // 9) // 16 * 16, 1)
    higher = list(range(2, bits))
    first = scatter_sum(stacked[..., :cut, :], [0, "samp", 1] + higher)
    second = scatter_sum(stacked[..., cut:, :], [0, 1, "samp"] + higher)
    return jnp.concatenate([first, second], axis=0).astype(jnp.float32)


def per_device(trunk, conv_weight, head_weight, targets, error_mask, upweight):
    windows, positions, channels = trunk.shape
    row_count = windows * positions
    bins_all = row_count * lax.axis_size("seq") * lax.axis_size("samp")
    bin_weight = jnp.where(error_mask == 1, upweight, 1).astype(jnp.float32)
    weight_sum = lax.psum(jnp.sum(bin_weight), ("seq", "samp"))
    stream = trunk
    stored = []
    padded_acts = []
    for layer_number in range(LAYERS):
        spread = BASE_DILATION * 2**layer_number
        activated = smooth(stream.astype(jnp.float32)).astype(jnp.bfloat16)
        padded = extended(activated, spread)
        taps = jnp.concatenate(
            [padded[:, k * spread : k * spread + positions] for k in range(3)], axis=2
        ).reshape(row_count, 3 * channels)
        conv_out = jnp.dot(
            taps,
            conv_weight[layer_number].reshape(3 * channels, channels),
            preferred_element_type=jnp.float32,
        )
        stored.append(stream)
        padded_acts.append(taps)
        stream = (stream.astype(jnp.float32) + conv_out.reshape(stream.shape)).astype(jnp.bfloat16)
    residual_rows = stream.reshape(row_count, channels)
    logits = jnp.dot(residual_rows, head_weight, preferred_element_type=jnp.float32)
    predicted = jax.nn.softplus(logits)
    slope = jax.nn.sigmoid(logits)
    counts = targets.reshape(row_count, -1).astype(jnp.float32)
    flat_weight = bin_weight.reshape(row_count, 1)
    partial_loss = jnp.sum(flat_weight * (predicted - counts * jnp.log(predicted)))
    loss_sum = lax.psum(partial_loss, ("seq", "samp"))
    factor = bins_all / weight_sum
    logit_grad = (factor * flat_weight * (1.0 - counts / predicted) * slope).astype(jnp.bfloat16)
    half = logit_grad.shape[1] // 2
    head_total = reduced(
        [
            jnp.dot(residual_rows.T, part, preferred_element_type=jnp.float32).astype(jnp.bfloat16)
            for part in (logit_grad[:, :half], logit_grad[:, half:])
        ]
    )
    stream_grad = jnp.dot(logit_grad, head_weight.T, preferred_element_type=jnp.float32).reshape(
        windows, positions, channels
    )
    kernel_grads = [None] * LAYERS
    for layer_number in reversed(range(LAYERS)):
        spread = BASE_DILATION * 2**layer_number
        grad_bf = stream_grad.astype(jnp.bfloat16)
        grad_flat = grad_bf.reshape(row_count, channels)
        padded_grad = extended(grad_bf, spread)
        side = channels // 2
        kernel_grads[layer_number] = reduced(
            [
                jnp.dot(
                    padded_acts[layer_number].T, part, preferred_element_type=jnp.float32
                ).astype(jnp.bfloat16)
                for part in (grad_flat[:, :side], grad_flat[:, side:])
            ]
        )
        act_grad = jnp.zeros((row_count, channels), jnp.float32)
        for k in range(3):
            view = padded_grad[:, (2 - k) * spread : (2 - k) * spread + positions]
            act_grad = act_grad + jnp.dot(
                view.reshape(row_count, channels),
                conv_weight[layer_number, k].T,
                preferred_element_type=jnp.float32,
            )
        residual_float32 = stored[layer_number].astype(jnp.float32)
        pullback = jax.vjp(smooth, residual_float32)[1]
        stream_grad = stream_grad + pullback(act_grad.reshape(residual_float32.shape))[0]
    loss = loss_sum / (OUTPUT_TRACKS * weight_sum)
    return (loss, jnp.stack(kernel_grads), head_total, stream_grad.astype(jnp.bfloat16))


MESH = pl.DeviceIdType.MESH
TILE = 384
ORDERS = (
    (("samp", 1, 2, 3), (1, "samp", 2, 3), (2, 3, "samp", 1)),
    ((1, 2, 3), (1, 2, 3), (1, 2, 3)),
    ((1, 2, 3), (2, 3, 1)),
    ((1, 2, 3), (2, 3, 1)),
)
LABELS = (("samp", 3, 2, 1), (3, 2, 1), (3, 2, 1), (3, 2, 1))
CUTS = ((0, 16, 32, 48), (0, 48, 96, 144), (0, 128, 144), (0, 80, 144))
CHUNKS = LAYERS + 1
TURNS = {
    0: (
    ),
    3: (
    ),
    2: (
        (0, 0, 0), (0, 1, 0), (0, 2, 0), (3, 1, 0), (3, 0, 0),
    ),
    1: (
        (2, 1, 0), (0, 1, 1), (0, 2, 1), (3, 1, 1), (2, 0, 0), (3, 0, 1),
        (2, 1, 1), (0, 2, 2), (0, 0, 1), (0, 1, 2), (1, 0, 0), (2, 0, 1),
        (3, 0, 2), (1, 1, 0), (0, 0, 2), (0, 1, 3), (1, 2, 0), (1, 0, 1),
        (3, 1, 2), (2, 1, 2), (0, 2, 3), (2, 0, 2), (1, 1, 1), (0, 0, 3),
        (1, 2, 1), (1, 0, 2), (1, 1, 2), (1, 2, 2),
    ),
}
SLOTS = tuple(
    (chunk, part, step)
    for chunk in range(CHUNKS)
    for part in range(len(ORDERS[chunk]))
    for step in range(len(LABELS[chunk]))
)
FIRST = 8 * LAYERS
LATER = FIRST + CHUNKS
LOSS = LATER + len(SLOTS)
COPIES = LOSS + 5


def smooth_slope(values):
    scale = 0.7978845608028654
    square = values * values
    bend = jnp.tanh(scale * values * (1.0 + 0.044715 * square))
    return 0.5 * (1.0 + bend) + 0.5 * values * (1.0 - bend * bend) * scale * (
        1.0 + 3 * 0.044715 * square
    )


def dot(left, right, left_dim, right_dim):
    return lax.dot_general(
        left, right, (((left_dim,), (right_dim,)), ((), ())), preferred_element_type=jnp.float32
    )


def kernel(
    trunk, conv_hbm, head_hbm, targets_hbm, mask, upweight, loss_out, conv_out, head_out, trunk_out, *scratch
):
    conv_w, head_w, counts, local_sem, send_sem, recv_sem, acts, grads, streams, slopes = scratch[:10]
    stream_grad, weights, sums, turned, other_acts, other_grads = scratch[10:16]
    scratch = scratch[5:]
    terms, first, later, loss_slots = (
        scratch[11 : 11 + CHUNKS],
        scratch[11 + CHUNKS : 11 + 2 * CHUNKS],
        scratch[11 + 2 * CHUNKS : -1],
        scratch[-1],
    )
    rows, channels = trunk.shape
    tracks = head_hbm.shape[1]
    seq, samp = lax.axis_index("seq"), lax.axis_index("samp")
    last = lax.axis_size("seq") - 1
    has_left, has_right = seq > 0, seq < last
    bits = [lax.rem(lax.div(seq, 2**b), 2) for b in range(4)]
    place = {"samp": samp, **{b: bits[b] for b in range(4)}}
    partner = {"samp": {"samp": 1 - samp}}
    for b in range(4):
        partner[b] = {"seq": seq + (1 - 2 * bits[b]) * 2**b}

    conv_loads = [
        pltpu.make_async_copy(conv_hbm.at[i], conv_w.at[i], local_sem.at[i]) for i in range(LAYERS)
    ]
    head_load = pltpu.make_async_copy(head_hbm, head_w, local_sem.at[LAYERS])
    count_load = pltpu.make_async_copy(targets_hbm, counts, local_sem.at[LAYERS + 1])
    for load in conv_loads + [head_load, count_load]:
        load.start()

    streams[0] = trunk[...]
    first_act = smooth(trunk[...].astype(jnp.float32)).astype(jnp.bfloat16)
    row = jnp.where(mask[...] == 1, upweight[...], 1).astype(jnp.float32)
    weights[...] = jnp.broadcast_to(row, (128, rows)).T

    barrier = pltpu.get_barrier_semaphore()
    right, left = {"seq": seq + 1}, {"seq": seq - 1}
    for there in (partner["samp"], partner[1], partner[2], partner[3]):
        pl.semaphore_signal(barrier, inc=1, device_id=there, device_id_type=MESH)

    @pl.when(has_right)
    def _():
        pl.semaphore_signal(barrier, inc=1, device_id=right, device_id_type=MESH)

    @pl.when(has_left)
    def _():
        pl.semaphore_signal(barrier, inc=1, device_id=left, device_id_type=MESH)

    pl.semaphore_wait(barrier, 4 + has_right.astype(jnp.int32) + has_left.astype(jnp.int32))

    def remote(src, dst, number, there):
        return pltpu.make_async_remote_copy(
            src_ref=src,
            dst_ref=dst,
            send_sem=send_sem.at[number],
            recv_sem=recv_sem.at[number],
            device_id=there,
            device_id_type=MESH,
        )

    spreads = [BASE_DILATION * 2**i for i in range(LAYERS)]
    starts = [sum(rows + 2 * s for s in spreads[:i]) for i in range(LAYERS)]

    def edges(buffer, layer, number):
        spread, start = spreads[layer], starts[layer]
        up = remote(
            buffer.at[pl.ds(start + rows, spread)], buffer.at[pl.ds(start, spread)], number, right
        )
        down = remote(
            buffer.at[pl.ds(start + spread, spread)],
            buffer.at[pl.ds(start + spread + rows, spread)],
            number + 1,
            left,
        )
        return up, down

    def send_edges(buffer, layer, number):
        spread, start = spreads[layer], starts[layer]
        up, down = edges(buffer, layer, number)

        @pl.when(has_right)
        def _():
            up.start()

        @pl.when(has_left)
        def _():
            down.start()

        @pl.when(jnp.logical_not(has_left))
        def _():
            buffer[pl.ds(start, spread)] = jnp.zeros((spread, channels), jnp.bfloat16)

        @pl.when(jnp.logical_not(has_right))
        def _():
            buffer[pl.ds(start + spread + rows, spread)] = jnp.zeros((spread, channels), jnp.bfloat16)

    def wait_edges(buffer, layer, number):
        up, down = edges(buffer, layer, number)

        @pl.when(has_right)
        def _():
            up.wait_send()
            down.wait_recv()

        @pl.when(has_left)
        def _():
            down.wait_send()
            up.wait_recv()

    def view(buffer, layer, tap):
        return buffer[pl.ds(starts[layer] + tap * spreads[layer], rows)]

    side = channels // 2
    my_side = pl.ds(pl.multiple_of(samp * side, 128), side)
    other_side = pl.ds(pl.multiple_of((1 - samp) * side, 128), side)

    def middle_rows(layer):
        return pl.ds(starts[layer] + spreads[layer], rows)

    def act_copy(layer):
        place_of = middle_rows(layer)
        return remote(
            acts.at[place_of], other_acts.at[place_of], 8 * layer + 6, partner["samp"]
        )

    def grad_copy(layer):
        return remote(
            grads.at[middle_rows(layer), other_side],
            other_grads.at[layer],
            8 * layer + 7,
            partner["samp"],
        )

    for layer in range(LAYERS):
        block = first_act
        if layer > 0:
            block = smooth(streams[layer].astype(jnp.float32)).astype(jnp.bfloat16)
        acts[middle_rows(layer)] = block
        send_edges(acts, layer, 8 * layer)
        act_copy(layer).start()
        conv_loads[layer].wait()
        total = streams[layer].astype(jnp.float32) + dot(view(acts, layer, 1), conv_w[layer, 1], 1, 0)
        wait_edges(acts, layer, 8 * layer)
        for tap in (0, 2):
            total += dot(view(acts, layer, tap), conv_w[layer, tap], 1, 0)
        streams[layer + 1] = total.astype(jnp.bfloat16)
        if layer > 0:
            act_copy(layer - 1).wait()
            send_edges(other_acts, layer - 1, 8 * (layer - 1) + 2)

    head_load.wait()
    count_load.wait()
    turned[...] = streams[LAYERS][...].T

    def folded(values):
        return jnp.sum(values.reshape(rows // 8, 8, values.shape[1]), axis=0)

    def first_copy(chunk):
        return remote(
            terms[chunk].at[(slice(None),) * len(LABELS[chunk]) + (1 - bits[0],)],
            first[chunk],
            FIRST + chunk,
            partner[0],
        )

    def part_rows(chunk, part):
        return pl.ds(CUTS[chunk][part], CUTS[chunk][part + 1] - CUTS[chunk][part])

    def slot(chunk, part, step):
        return later[SLOTS.index((chunk, part, step))]

    def picked(chunk, part, step, which):
        order = ORDERS[chunk][part]
        labels = list(LABELS[chunk])
        for done in order[:step]:
            labels.remove(done)
        dim = labels.index(order[step])
        index = place[order[step]] if which == 0 else 1 - place[order[step]]
        return labels, dim, index

    def later_copy(chunk, part, step):
        labels, dim, index = picked(chunk, part, step, 1)
        at = [slice(None)] * len(labels)
        at[dim] = index
        if step == 0:
            src = first[chunk].at[tuple(at) + (part_rows(chunk, part),)]
        else:
            src = slot(chunk, part, step - 1).at[tuple(at)]
        number = LATER + SLOTS.index((chunk, part, step))
        return remote(src, slot(chunk, part, step), number, partner[ORDERS[chunk][part][step]])

    def added(a, b):
        return a.astype(jnp.float32) + b.astype(jnp.float32)

    def digits(number, count):
        return tuple(lax.rem(lax.div(number, 2 ** (count - 1 - i)), 2) for i in range(count))

    def start_later(chunk):
        first_copy(chunk).wait()

        def add(number, carry):
            at = digits(number, len(LABELS[chunk]))
            first[chunk][at] = added(first[chunk][at], terms[chunk][at + (bits[0],)]).astype(
                jnp.bfloat16
            )
            return carry

        lax.fori_loop(0, 2 ** len(LABELS[chunk]), add, 0)
        for part in range(len(ORDERS[chunk])):
            later_copy(chunk, part, 0).start()

    def advance(chunk, part, step):
        later_copy(chunk, part, step).wait()
        labels, dim, index = picked(chunk, part, step, 0)
        held = slot(chunk, part, step)
        before = first[chunk] if step == 0 else slot(chunk, part, step - 1)
        count = len(labels) - 1

        def values(at):
            there = at[:dim] + (index,) + at[dim:]
            if step == 0:
                there = there + (part_rows(chunk, part),)
            return added(held[at] if at else held[...], before[there])

        if step == len(LABELS[chunk]) - 1:
            where = part_rows(chunk, part)
            total = values(()) * factor()
            if chunk == 0:
                half = head_out.shape[1]
                moved = pltpu.roll(total, half, axis=1)
                head_out[where] = jnp.where(samp == 1, moved, total)[:, :half]
            else:
                conv_out[chunk - 1, where] = total
        else:

            def add(number, carry):
                at = digits(number, count)
                held[at] = values(at).astype(jnp.bfloat16)
                return carry

            lax.fori_loop(0, 2**count, add, 0)
            later_copy(chunk, part, step + 1).start()

    def weight_sum():
        return jnp.sum(sums[8:16, 0:1], axis=0, keepdims=True)

    def factor():
        bins_all = float(rows) * lax.axis_size("seq") * lax.axis_size("samp")
        return bins_all / weight_sum()

    def loss_copy(step):
        there = partner[(0, "samp", 1, 2, 3)[step]]
        return remote(loss_slots.at[2 * step], loss_slots.at[2 * step + 1], LOSS + step, there)

    def loss_start(step):
        loss_slots[2 * step] = sums[...]
        loss_copy(step).start()

    def loss_end(step):
        loss_copy(step).wait()
        sums[...] += loss_slots[2 * step + 1]

    def put(chunk, value, row):
        size = terms[chunk].shape[4]
        at = 0
        while at < value.shape[0]:
            block, inner = divmod(row + at, size)
            length = min(size - inner, value.shape[0] - at)
            where = tuple((block >> b) & 1 for b in (3, 2, 1, 0))
            terms[chunk][where + (pl.ds(inner, length),)] = value[at : at + length].astype(jnp.bfloat16)
            at += length

    wide = terms[0].shape[6]
    loss_fold = jnp.zeros((8, 128), jnp.float32)
    for tile in range(tracks // TILE):
        begin = tile * TILE
        matrix = head_w[:, begin : begin + TILE]
        logits = dot(streams[LAYERS], matrix, 1, 0)
        weight = jnp.concatenate([weights[...]] * (TILE // 128), axis=1)
        tail = jnp.exp(-jnp.abs(logits))
        above = 1.0 + tail
        inverse = 1.0 / above
        predicted = jnp.maximum(logits, 0.0) + (jnp.log(above) + (tail - (above - 1.0)) * inverse)
        slope = jnp.where(logits >= 0, 1.0, tail) * inverse
        seen = counts[:, begin : begin + TILE].astype(jnp.float32)
        fold = folded(weight * (predicted - seen * jnp.log(predicted)))
        loss_fold += sum(fold[:, i * 128 : (i + 1) * 128] for i in range(TILE // 128))
        grad = (weight * (1.0 - seen / predicted) * slope).astype(jnp.bfloat16)
        slopes[:, begin : begin + TILE] = grad
        value = dot(turned[...], grad, 1, 0).astype(jnp.bfloat16)
        for side in range(2):
            base = side * (tracks - wide)
            low, high = max(begin, base), min(begin + TILE, base + wide)
            if low < high:
                for block in range(16):
                    where = (side,) + tuple((block >> b) & 1 for b in (3, 2, 1, 0))
                    terms[0][where + (slice(None), pl.ds(low - base, high - low))] = value[
                        block * 48 : (block + 1) * 48, low - begin : high - begin
                    ]
    first_copy(0).start()
    sums[0:8] = loss_fold
    sums[8:16] = folded(weights[...])
    loss_start(0)
    stream_grad[...] = dot(slopes[...], head_w[...], 1, 1)

    def send_grad(layer):
        grads[middle_rows(layer)] = stream_grad[...].astype(jnp.bfloat16)
        send_edges(grads, layer, 8 * layer + 4)
        grad_copy(layer).start()

    def begin_and_turn(chunk):
        start_later(chunk)
        for turn in TURNS[chunk]:
            advance(*turn)

    send_grad(LAYERS - 1)
    act_copy(LAYERS - 1).wait()
    send_edges(other_acts, LAYERS - 1, 8 * (LAYERS - 1) + 2)
    chunk = 0
    for layer in reversed(range(LAYERS)):
        total = dot(view(grads, layer, 1), conv_w[layer, 1], 1, 1)
        begin_and_turn(chunk)
        chunk = layer + 1
        wait_edges(grads, layer, 8 * layer + 4)
        for tap in (0, 2):
            total += dot(view(grads, layer, 2 - tap), conv_w[layer, tap], 1, 1)
        stream_grad[...] += smooth_slope(streams[layer].astype(jnp.float32)) * total
        if layer > 0:
            send_grad(layer - 1)
        loss_end(LAYERS - 1 - layer)
        loss_start(LAYERS - layer)
        wait_edges(other_acts, layer, 8 * layer + 2)
        grad_copy(layer).wait()
        both = jnp.concatenate([grads[middle_rows(layer), my_side], other_grads[layer]], axis=0)
        for tap in range(3):
            place_of = pl.ds(starts[layer] + tap * spreads[layer], rows)
            for begin in range(0, channels, 384):
                seen = jnp.concatenate(
                    [
                        acts[place_of, begin : begin + 384],
                        other_acts[place_of, begin : begin + 384],
                    ],
                    axis=0,
                )
                put(layer + 1, dot(seen, both, 0, 0), tap * channels + begin)
        first_copy(layer + 1).start()
    loss_end(3)
    loss_start(4)
    start_later(1)
    loss_end(4)
    trunk_out[...] = (stream_grad[...] * factor()).astype(jnp.bfloat16)
    loss_out[...] = jnp.sum(
        jnp.sum(sums[0:8], axis=0, keepdims=True), axis=1, keepdims=True
    ) / (OUTPUT_TRACKS * weight_sum())
    for turn in TURNS[1]:
        advance(*turn)


def per_device_kernel(trunk, conv_weight, head_weight, targets, error_mask, upweight):
    windows, rows, channels = trunk.shape
    devices = lax.axis_size("seq")
    tracks = head_weight.shape[1]
    spreads = [BASE_DILATION * 2**i for i in range(LAYERS)]
    extended_rows = sum(rows + 2 * s for s in spreads)
    half = tracks // 2
    wide = (half + 127) // 128 * 128
    sizes = [(channels // devices, wide)] + [(3 * channels // devices, channels // 2)] * LAYERS
    vmem = functools.partial(pltpu.VMEM, dtype=jnp.bfloat16)
    scratch = [
        vmem(conv_weight.shape),
        vmem(head_weight.shape),
        pltpu.VMEM((rows, tracks), jnp.int32),
        pltpu.SemaphoreType.DMA((LAYERS + 2,)),
        pltpu.SemaphoreType.DMA((COPIES,)),
        pltpu.SemaphoreType.DMA((COPIES,)),
        vmem((extended_rows, channels)),
        vmem((extended_rows, channels)),
        vmem((LAYERS + 1, rows, channels)),
        vmem((rows, tracks)),
        pltpu.VMEM((rows, channels), jnp.float32),
        pltpu.VMEM((rows, 128), jnp.float32),
        pltpu.VMEM((16, 128), jnp.float32),
        vmem((channels, rows)),
        vmem((extended_rows, channels)),
        vmem((LAYERS, rows, channels // 2)),
    ]
    counts = [len(labels) for labels in LABELS]
    scratch += [vmem((2,) * (count + 1) + size) for count, size in zip(counts, sizes)]
    scratch += [vmem((2,) * count + size) for count, size in zip(counts, sizes)]
    for chunk, part, step in SLOTS:
        part_rows = CUTS[chunk][part + 1] - CUTS[chunk][part]
        scratch.append(vmem((2,) * (counts[chunk] - 1 - step) + (part_rows, sizes[chunk][1])))
    scratch.append(pltpu.VMEM((10, 16, 128), jnp.float32))
    whole = pl.BlockSpec(memory_space=pltpu.VMEM)
    away = pl.BlockSpec(memory_space=pl.ANY)
    loss, conv_grad, head_grad, trunk_grad = pl.pallas_call(
        kernel,
        out_shape=(
            jax.ShapeDtypeStruct((1, 1), jnp.float32),
            jax.ShapeDtypeStruct((LAYERS,) + sizes[1], jnp.float32),
            jax.ShapeDtypeStruct((sizes[0][0], half), jnp.float32),
            jax.ShapeDtypeStruct((rows, channels), jnp.bfloat16),
        ),
        in_specs=[whole, away, away, away, whole, whole],
        out_specs=(whole,) * 4,
        scratch_shapes=scratch,
        compiler_params=pltpu.CompilerParams(
            collective_id=0, has_side_effects=True, vmem_limit_bytes=63 * 2**20
        ),
    )(
        trunk.reshape(rows, channels),
        conv_weight,
        head_weight,
        targets.reshape(rows, tracks),
        error_mask,
        upweight,
    )
    return loss.reshape(()), conv_grad, head_grad, trunk_grad.reshape(trunk.shape)


def fits(mesh):
    return mesh.shape["seq"] == 16 and mesh.shape["samp"] == 2


def solution(mesh):
    return jax.shard_map(
        per_device_kernel if fits(mesh) else per_device,
        mesh=mesh,
        in_specs=(
            P("samp", "seq", None),
            P(),
            P(),
            P("samp", "seq", None),
            P("samp", "seq"),
            P("samp", "seq"),
        ),
        out_specs=(P(), P(None, "seq", "samp"), P("seq", "samp"), P("samp", "seq", None)),
        check_vma=False,
    )
```

```python
import functools

import jax
import jax.numpy as jnp
from jax import lax
from jax.experimental import pallas as pl
from jax.experimental.pallas import tpu as pltpu
from jax.sharding import PartitionSpec as P

OUTPUT_TRACKS = 2688
LAYERS = 3
BASE_DILATION = 64


def extended(shard, width):
    devices, length = (lax.axis_size("seq"), shard.shape[1])
    up = [(i, (i + 1) % devices) for i in range(devices - 1)]
    down = [(j, i) for i, j in up]
    before = lax.ppermute(lax.slice_in_dim(shard, length - width, length, axis=1), "seq", up)
    after = lax.ppermute(lax.slice_in_dim(shard, 0, width, axis=1), "seq", down)
    return jnp.concatenate([before, shard, after], axis=1)


def smooth(values):
    return jax.nn.gelu(values, approximate=True)


def halve(part, dim, axis, bit):
    place = lax.axis_index(axis)
    mine = lax.rem(lax.div(place, 2**bit), 2)
    pairs = [(i, i ^ (2**bit)) for i in range(lax.axis_size(axis))]
    away = lax.dynamic_index_in_dim(part, 1 - mine, dim, keepdims=False)
    kept = lax.dynamic_index_in_dim(part, mine, dim, keepdims=False)
    come = lax.ppermute(away, axis, pairs)
    return (kept.astype(jnp.float32) + come.astype(jnp.float32)).astype(jnp.bfloat16)


def scatter_sum(part, order):
    labels = ["samp"] + list(reversed(range(part.ndim - 3)))
    for step in order:
        dim = labels.index(step)
        part = halve(part, dim, *(("samp", 0) if step == "samp" else ("seq", step)))
        labels.pop(dim)
    return part


def reduced(halves):
    devices = lax.axis_size("seq")
    bits = devices.bit_length() - 1
    rows = halves[0].shape[0] // devices
    stacked = jnp.stack([h.reshape((2,) * bits + (rows, h.shape[1])) for h in halves], axis=0)
    cut = max((rows * 5 // 9) // 16 * 16, 1)
    higher = list(range(2, bits))
    first = scatter_sum(stacked[..., :cut, :], [0, "samp", 1] + higher)
    second = scatter_sum(stacked[..., cut:, :], [0, 1, "samp"] + higher)
    return jnp.concatenate([first, second], axis=0).astype(jnp.float32)


def per_device(trunk, conv_weight, head_weight, targets, error_mask, upweight):
    windows, positions, channels = trunk.shape
    row_count = windows * positions
    bins_all = row_count * lax.axis_size("seq") * lax.axis_size("samp")
    bin_weight = jnp.where(error_mask == 1, upweight, 1).astype(jnp.float32)
    weight_sum = lax.psum(jnp.sum(bin_weight), ("seq", "samp"))
    stream = trunk
    stored = []
    padded_acts = []
    for layer_number in range(LAYERS):
        spread = BASE_DILATION * 2**layer_number
        activated = smooth(stream.astype(jnp.float32)).astype(jnp.bfloat16)
        padded = extended(activated, spread)
        taps = jnp.concatenate(
            [padded[:, k * spread : k * spread + positions] for k in range(3)], axis=2
        ).reshape(row_count, 3 * channels)
        conv_out = jnp.dot(
            taps,
            conv_weight[layer_number].reshape(3 * channels, channels),
            preferred_element_type=jnp.float32,
        )
        stored.append(stream)
        padded_acts.append(taps)
        stream = (stream.astype(jnp.float32) + conv_out.reshape(stream.shape)).astype(jnp.bfloat16)
    residual_rows = stream.reshape(row_count, channels)
    logits = jnp.dot(residual_rows, head_weight, preferred_element_type=jnp.float32)
    predicted = jax.nn.softplus(logits)
    slope = jax.nn.sigmoid(logits)
    counts = targets.reshape(row_count, -1).astype(jnp.float32)
    flat_weight = bin_weight.reshape(row_count, 1)
    partial_loss = jnp.sum(flat_weight * (predicted - counts * jnp.log(predicted)))
    loss_sum = lax.psum(partial_loss, ("seq", "samp"))
    factor = bins_all / weight_sum
    logit_grad = (factor * flat_weight * (1.0 - counts / predicted) * slope).astype(jnp.bfloat16)
    half = logit_grad.shape[1] // 2
    head_total = reduced(
        [
            jnp.dot(residual_rows.T, part, preferred_element_type=jnp.float32).astype(jnp.bfloat16)
            for part in (logit_grad[:, :half], logit_grad[:, half:])
        ]
    )
    stream_grad = jnp.dot(logit_grad, head_weight.T, preferred_element_type=jnp.float32).reshape(
        windows, positions, channels
    )
    kernel_grads = [None] * LAYERS
    for layer_number in reversed(range(LAYERS)):
        spread = BASE_DILATION * 2**layer_number
        grad_bf = stream_grad.astype(jnp.bfloat16)
        grad_flat = grad_bf.reshape(row_count, channels)
        padded_grad = extended(grad_bf, spread)
        side = channels // 2
        kernel_grads[layer_number] = reduced(
            [
                jnp.dot(
                    padded_acts[layer_number].T, part, preferred_element_type=jnp.float32
                ).astype(jnp.bfloat16)
                for part in (grad_flat[:, :side], grad_flat[:, side:])
            ]
        )
        act_grad = jnp.zeros((row_count, channels), jnp.float32)
        for k in range(3):
            view = padded_grad[:, (2 - k) * spread : (2 - k) * spread + positions]
            act_grad = act_grad + jnp.dot(
                view.reshape(row_count, channels),
                conv_weight[layer_number, k].T,
                preferred_element_type=jnp.float32,
            )
        residual_float32 = stored[layer_number].astype(jnp.float32)
        pullback = jax.vjp(smooth, residual_float32)[1]
        stream_grad = stream_grad + pullback(act_grad.reshape(residual_float32.shape))[0]
    loss = loss_sum / (OUTPUT_TRACKS * weight_sum)
    return (loss, jnp.stack(kernel_grads), head_total, stream_grad.astype(jnp.bfloat16))


MESH = pl.DeviceIdType.MESH
TILE = 384
ORDERS = (
    (("samp", 1, 2, 3), (1, "samp", 2, 3), (2, 3, "samp", 1)),
    ((1, 2, 3), (1, 2, 3)),
    ((1, 2, 3), (2, 3, 1)),
    ((1, 2, 3), (2, 3, 1)),
)
LABELS = (("samp", 3, 2, 1), (3, 2, 1), (3, 2, 1), (3, 2, 1))
CUTS = ((0, 16, 32, 48), (0, 80, 144), (0, 80, 144), (0, 64, 144))
CHUNKS = LAYERS + 1
TURNS = {
    0: (
    ),
    3: (
    ),
    2: (
        (0, 2, 0), (0, 0, 0), (0, 1, 0), (3, 1, 0),
    ),
    1: (
        (3, 0, 0), (2, 1, 0), (2, 0, 0), (0, 1, 1), (0, 2, 1), (3, 1, 1),
        (0, 0, 1), (3, 0, 1), (0, 2, 2), (2, 1, 1), (1, 0, 0), (2, 0, 1),
        (0, 1, 2), (1, 1, 0), (0, 0, 2), (3, 1, 2), (3, 0, 2), (0, 2, 3),
        (2, 1, 2), (1, 0, 1), (2, 0, 2), (0, 1, 3), (1, 1, 1), (0, 0, 3),
        (1, 0, 2), (1, 1, 2),
    ),
}
SLOTS = tuple(
    (chunk, part, step)
    for chunk in range(CHUNKS)
    for part in range(len(ORDERS[chunk]))
    for step in range(len(LABELS[chunk]))
)
FIRST = 8 * LAYERS
LATER = FIRST + CHUNKS
LOSS = LATER + len(SLOTS)
COPIES = LOSS + 5


def smooth_slope(values):
    scale = 0.7978845608028654
    square = values * values
    bend = jnp.tanh(scale * values * (1.0 + 0.044715 * square))
    return 0.5 * (1.0 + bend) + 0.5 * values * (1.0 - bend * bend) * scale * (
        1.0 + 3 * 0.044715 * square
    )


def dot(left, right, left_dim, right_dim):
    return lax.dot_general(
        left, right, (((left_dim,), (right_dim,)), ((), ())), preferred_element_type=jnp.float32
    )


def kernel(
    trunk, conv_hbm, head_hbm, targets_hbm, mask, upweight, loss_out, conv_out, head_out, trunk_out, *scratch
):
    conv_w, head_w, counts, local_sem, send_sem, recv_sem, acts, grads, streams, slopes = scratch[:10]
    stream_grad, weights, sums, turned, other_acts, other_grads = scratch[10:16]
    scratch = scratch[5:]
    terms, first, later, loss_slots = (
        scratch[11 : 11 + CHUNKS],
        scratch[11 + CHUNKS : 11 + 2 * CHUNKS],
        scratch[11 + 2 * CHUNKS : -1],
        scratch[-1],
    )
    rows, channels = trunk.shape
    tracks = head_hbm.shape[1]
    seq, samp = lax.axis_index("seq"), lax.axis_index("samp")
    last = lax.axis_size("seq") - 1
    has_left, has_right = seq > 0, seq < last
    bits = [lax.rem(lax.div(seq, 2**b), 2) for b in range(4)]
    place = {"samp": samp, **{b: bits[b] for b in range(4)}}
    partner = {"samp": {"samp": 1 - samp}}
    for b in range(4):
        partner[b] = {"seq": seq + (1 - 2 * bits[b]) * 2**b}

    conv_loads = [
        pltpu.make_async_copy(conv_hbm.at[i], conv_w.at[i], local_sem.at[i]) for i in range(LAYERS)
    ]
    head_load = pltpu.make_async_copy(head_hbm, head_w, local_sem.at[LAYERS])
    count_load = pltpu.make_async_copy(targets_hbm, counts, local_sem.at[LAYERS + 1])
    for load in conv_loads + [head_load, count_load]:
        load.start()

    streams[0] = trunk[...]
    first_act = smooth(trunk[...].astype(jnp.float32)).astype(jnp.bfloat16)
    row = jnp.where(mask[...] == 1, upweight[...], 1).astype(jnp.float32)
    weights[...] = jnp.broadcast_to(row, (128, rows)).T

    barrier = pltpu.get_barrier_semaphore()
    right, left = {"seq": seq + 1}, {"seq": seq - 1}
    for there in (partner["samp"], partner[1], partner[2], partner[3]):
        pl.semaphore_signal(barrier, inc=1, device_id=there, device_id_type=MESH)

    @pl.when(has_right)
    def _():
        pl.semaphore_signal(barrier, inc=1, device_id=right, device_id_type=MESH)

    @pl.when(has_left)
    def _():
        pl.semaphore_signal(barrier, inc=1, device_id=left, device_id_type=MESH)

    pl.semaphore_wait(barrier, 4 + has_right.astype(jnp.int32) + has_left.astype(jnp.int32))

    def remote(src, dst, number, there):
        return pltpu.make_async_remote_copy(
            src_ref=src,
            dst_ref=dst,
            send_sem=send_sem.at[number],
            recv_sem=recv_sem.at[number],
            device_id=there,
            device_id_type=MESH,
        )

    spreads = [BASE_DILATION * 2**i for i in range(LAYERS)]
    starts = [sum(rows + 2 * s for s in spreads[:i]) for i in range(LAYERS)]

    def edges(buffer, layer, number):
        spread, start = spreads[layer], starts[layer]
        up = remote(
            buffer.at[pl.ds(start + rows, spread)], buffer.at[pl.ds(start, spread)], number, right
        )
        down = remote(
            buffer.at[pl.ds(start + spread, spread)],
            buffer.at[pl.ds(start + spread + rows, spread)],
            number + 1,
            left,
        )
        return up, down

    def send_edges(buffer, layer, number):
        spread, start = spreads[layer], starts[layer]
        up, down = edges(buffer, layer, number)

        @pl.when(has_right)
        def _():
            up.start()

        @pl.when(has_left)
        def _():
            down.start()

        @pl.when(jnp.logical_not(has_left))
        def _():
            buffer[pl.ds(start, spread)] = jnp.zeros((spread, channels), jnp.bfloat16)

        @pl.when(jnp.logical_not(has_right))
        def _():
            buffer[pl.ds(start + spread + rows, spread)] = jnp.zeros((spread, channels), jnp.bfloat16)

    def wait_edges(buffer, layer, number):
        up, down = edges(buffer, layer, number)

        @pl.when(has_right)
        def _():
            up.wait_send()
            down.wait_recv()

        @pl.when(has_left)
        def _():
            down.wait_send()
            up.wait_recv()

    def view(buffer, layer, tap):
        return buffer[pl.ds(starts[layer] + tap * spreads[layer], rows)]

    side = channels // 2
    my_side = pl.ds(pl.multiple_of(samp * side, 128), side)
    other_side = pl.ds(pl.multiple_of((1 - samp) * side, 128), side)

    def middle_rows(layer):
        return pl.ds(starts[layer] + spreads[layer], rows)

    def act_copy(layer):
        place_of = middle_rows(layer)
        return remote(
            acts.at[place_of], other_acts.at[place_of], 8 * layer + 6, partner["samp"]
        )

    def grad_copy(layer):
        return remote(
            grads.at[middle_rows(layer), other_side],
            other_grads.at[layer],
            8 * layer + 7,
            partner["samp"],
        )

    for layer in range(LAYERS):
        block = first_act
        if layer > 0:
            block = smooth(streams[layer].astype(jnp.float32)).astype(jnp.bfloat16)
        acts[middle_rows(layer)] = block
        send_edges(acts, layer, 8 * layer)
        act_copy(layer).start()
        conv_loads[layer].wait()
        total = streams[layer].astype(jnp.float32) + dot(view(acts, layer, 1), conv_w[layer, 1], 1, 0)
        wait_edges(acts, layer, 8 * layer)
        for tap in (0, 2):
            total += dot(view(acts, layer, tap), conv_w[layer, tap], 1, 0)
        streams[layer + 1] = total.astype(jnp.bfloat16)

    for layer in reversed(range(LAYERS)):
        act_copy(layer).wait()
        send_edges(other_acts, layer, 8 * layer + 2)

    head_load.wait()
    count_load.wait()
    turned[...] = streams[LAYERS][...].T

    def folded(values):
        return jnp.sum(values.reshape(rows // 8, 8, values.shape[1]), axis=0)

    def first_copy(chunk):
        return remote(
            terms[chunk].at[(slice(None),) * len(LABELS[chunk]) + (1 - bits[0],)],
            first[chunk],
            FIRST + chunk,
            partner[0],
        )

    def part_rows(chunk, part):
        return pl.ds(CUTS[chunk][part], CUTS[chunk][part + 1] - CUTS[chunk][part])

    def slot(chunk, part, step):
        return later[SLOTS.index((chunk, part, step))]

    def picked(chunk, part, step, which):
        order = ORDERS[chunk][part]
        labels = list(LABELS[chunk])
        for done in order[:step]:
            labels.remove(done)
        dim = labels.index(order[step])
        index = place[order[step]] if which == 0 else 1 - place[order[step]]
        return labels, dim, index

    def later_copy(chunk, part, step):
        labels, dim, index = picked(chunk, part, step, 1)
        at = [slice(None)] * len(labels)
        at[dim] = index
        if step == 0:
            src = first[chunk].at[tuple(at) + (part_rows(chunk, part),)]
        else:
            src = slot(chunk, part, step - 1).at[tuple(at)]
        number = LATER + SLOTS.index((chunk, part, step))
        return remote(src, slot(chunk, part, step), number, partner[ORDERS[chunk][part][step]])

    def added(a, b):
        return a.astype(jnp.float32) + b.astype(jnp.float32)

    def digits(number, count):
        return tuple(lax.rem(lax.div(number, 2 ** (count - 1 - i)), 2) for i in range(count))

    def start_later(chunk):
        first_copy(chunk).wait()

        def add(number, carry):
            at = digits(number, len(LABELS[chunk]))
            first[chunk][at] = added(first[chunk][at], terms[chunk][at + (bits[0],)]).astype(
                jnp.bfloat16
            )
            return carry

        lax.fori_loop(0, 2 ** len(LABELS[chunk]), add, 0)
        for part in range(len(ORDERS[chunk])):
            later_copy(chunk, part, 0).start()

    def advance(chunk, part, step):
        later_copy(chunk, part, step).wait()
        labels, dim, index = picked(chunk, part, step, 0)
        held = slot(chunk, part, step)
        before = first[chunk] if step == 0 else slot(chunk, part, step - 1)
        count = len(labels) - 1

        def values(at):
            there = at[:dim] + (index,) + at[dim:]
            if step == 0:
                there = there + (part_rows(chunk, part),)
            return added(held[at] if at else held[...], before[there])

        if step == len(LABELS[chunk]) - 1:
            where = part_rows(chunk, part)
            total = values(()) * factor()
            if chunk == 0:
                half = head_out.shape[1]
                moved = pltpu.roll(total, half, axis=1)
                head_out[where] = jnp.where(samp == 1, moved, total)[:, :half]
            else:
                conv_out[chunk - 1, where] = total
        else:

            def add(number, carry):
                at = digits(number, count)
                held[at] = values(at).astype(jnp.bfloat16)
                return carry

            lax.fori_loop(0, 2**count, add, 0)
            later_copy(chunk, part, step + 1).start()

    def weight_sum():
        return jnp.sum(sums[8:16, 0:1], axis=0, keepdims=True)

    def factor():
        bins_all = float(rows) * lax.axis_size("seq") * lax.axis_size("samp")
        return bins_all / weight_sum()

    def loss_copy(step):
        there = partner[(0, "samp", 1, 2, 3)[step]]
        return remote(loss_slots.at[2 * step], loss_slots.at[2 * step + 1], LOSS + step, there)

    def loss_start(step):
        loss_slots[2 * step] = sums[...]
        loss_copy(step).start()

    def loss_end(step):
        loss_copy(step).wait()
        sums[...] += loss_slots[2 * step + 1]

    def put(chunk, value, row):
        size = terms[chunk].shape[4]
        at = 0
        while at < value.shape[0]:
            block, inner = divmod(row + at, size)
            length = min(size - inner, value.shape[0] - at)
            where = tuple((block >> b) & 1 for b in (3, 2, 1, 0))
            terms[chunk][where + (pl.ds(inner, length),)] = value[at : at + length].astype(jnp.bfloat16)
            at += length

    wide = terms[0].shape[6]
    loss_fold = jnp.zeros((8, 128), jnp.float32)
    for tile in range(tracks // TILE):
        begin = tile * TILE
        matrix = head_w[:, begin : begin + TILE]
        logits = dot(streams[LAYERS], matrix, 1, 0)
        weight = jnp.concatenate([weights[...]] * (TILE // 128), axis=1)
        tail = jnp.exp(-jnp.abs(logits))
        above = 1.0 + tail
        inverse = 1.0 / above
        predicted = jnp.maximum(logits, 0.0) + (jnp.log(above) + (tail - (above - 1.0)) * inverse)
        slope = jnp.where(logits >= 0, 1.0, tail) * inverse
        seen = counts[:, begin : begin + TILE].astype(jnp.float32)
        fold = folded(weight * (predicted - seen * jnp.log(predicted)))
        loss_fold += sum(fold[:, i * 128 : (i + 1) * 128] for i in range(TILE // 128))
        grad = (weight * (1.0 - seen / predicted) * slope).astype(jnp.bfloat16)
        slopes[:, begin : begin + TILE] = grad
        value = dot(turned[...], grad, 1, 0).astype(jnp.bfloat16)
        for side in range(2):
            base = side * (tracks - wide)
            low, high = max(begin, base), min(begin + TILE, base + wide)
            if low < high:
                for block in range(16):
                    where = (side,) + tuple((block >> b) & 1 for b in (3, 2, 1, 0))
                    terms[0][where + (slice(None), pl.ds(low - base, high - low))] = value[
                        block * 48 : (block + 1) * 48, low - begin : high - begin
                    ]
    first_copy(0).start()
    sums[0:8] = loss_fold
    sums[8:16] = folded(weights[...])
    loss_start(0)
    stream_grad[...] = dot(slopes[...], head_w[...], 1, 1)

    def send_grad(layer):
        grads[middle_rows(layer)] = stream_grad[...].astype(jnp.bfloat16)
        grad_copy(layer).start()
        send_edges(grads, layer, 8 * layer + 4)

    def begin_and_turn(chunk):
        start_later(chunk)
        for turn in TURNS[chunk]:
            advance(*turn)

    send_grad(LAYERS - 1)
    chunk = 0
    for layer in reversed(range(LAYERS)):
        begin_and_turn(chunk)
        chunk = layer + 1
        total = dot(view(grads, layer, 1), conv_w[layer, 1], 1, 1)
        wait_edges(other_acts, layer, 8 * layer + 2)
        grad_copy(layer).wait()
        both = jnp.concatenate([grads[middle_rows(layer), my_side], other_grads[layer]], axis=0)
        for tap in range(3):
            place_of = pl.ds(starts[layer] + tap * spreads[layer], rows)
            for begin in range(0, channels, 384):
                seen = jnp.concatenate(
                    [
                        acts[place_of, begin : begin + 384],
                        other_acts[place_of, begin : begin + 384],
                    ],
                    axis=0,
                )
                put(layer + 1, dot(seen, both, 0, 0), tap * channels + begin)
        first_copy(layer + 1).start()
        loss_end(LAYERS - 1 - layer)
        loss_start(LAYERS - layer)
        wait_edges(grads, layer, 8 * layer + 4)
        for tap in (0, 2):
            total += dot(view(grads, layer, 2 - tap), conv_w[layer, tap], 1, 1)
        stream_grad[...] += smooth_slope(streams[layer].astype(jnp.float32)) * total
        if layer > 0:
            send_grad(layer - 1)
    loss_end(3)
    loss_start(4)
    start_later(1)
    loss_end(4)
    trunk_out[...] = (stream_grad[...] * factor()).astype(jnp.bfloat16)
    loss_out[...] = jnp.sum(
        jnp.sum(sums[0:8], axis=0, keepdims=True), axis=1, keepdims=True
    ) / (OUTPUT_TRACKS * weight_sum())
    for turn in TURNS[1]:
        advance(*turn)


def settle(*refs):
    sources, targets, sems = refs[:3], refs[3:6], refs[6]
    copies = [
        pltpu.make_async_copy(a, b, sems.at[i]) for i, (a, b) in enumerate(zip(sources, targets))
    ]
    for copy in copies:
        copy.start()
    for copy in copies:
        copy.wait()


def per_device_kernel(trunk, conv_weight, head_weight, targets, error_mask, upweight):
    windows, rows, channels = trunk.shape
    devices = lax.axis_size("seq")
    tracks = head_weight.shape[1]
    spreads = [BASE_DILATION * 2**i for i in range(LAYERS)]
    extended_rows = sum(rows + 2 * s for s in spreads)
    half = tracks // 2
    wide = (half + 127) // 128 * 128
    sizes = [(channels // devices, wide)] + [(3 * channels // devices, channels // 2)] * LAYERS
    vmem = functools.partial(pltpu.VMEM, dtype=jnp.bfloat16)
    scratch = [
        vmem(conv_weight.shape),
        vmem(head_weight.shape),
        pltpu.VMEM((rows, tracks), jnp.int32),
        pltpu.SemaphoreType.DMA((LAYERS + 2,)),
        pltpu.SemaphoreType.DMA((COPIES,)),
        pltpu.SemaphoreType.DMA((COPIES,)),
        vmem((extended_rows, channels)),
        vmem((extended_rows, channels)),
        vmem((LAYERS + 1, rows, channels)),
        vmem((rows, tracks)),
        pltpu.VMEM((rows, channels), jnp.float32),
        pltpu.VMEM((rows, 128), jnp.float32),
        pltpu.VMEM((16, 128), jnp.float32),
        vmem((channels, rows)),
        vmem((extended_rows, channels)),
        vmem((LAYERS, rows, channels // 2)),
    ]
    counts = [len(labels) for labels in LABELS]
    scratch += [vmem((2,) * (count + 1) + size) for count, size in zip(counts, sizes)]
    scratch += [vmem((2,) * count + size) for count, size in zip(counts, sizes)]
    for chunk, part, step in SLOTS:
        part_rows = CUTS[chunk][part + 1] - CUTS[chunk][part]
        scratch.append(vmem((2,) * (counts[chunk] - 1 - step) + (part_rows, sizes[chunk][1])))
    scratch.append(pltpu.VMEM((10, 16, 128), jnp.float32))
    whole = pl.BlockSpec(memory_space=pltpu.VMEM)
    away = pl.BlockSpec(memory_space=pl.ANY)
    loss, conv_grad, head_grad, trunk_grad = pl.pallas_call(
        kernel,
        out_shape=(
            jax.ShapeDtypeStruct((1, 1), jnp.float32),
            jax.ShapeDtypeStruct((LAYERS,) + sizes[1], jnp.float32),
            jax.ShapeDtypeStruct((sizes[0][0], half), jnp.float32),
            jax.ShapeDtypeStruct((rows, channels), jnp.bfloat16),
        ),
        in_specs=[whole, away, away, away, whole, whole],
        out_specs=(whole,) * 4,
        scratch_shapes=scratch,
        compiler_params=pltpu.CompilerParams(
            collective_id=0, has_side_effects=True, vmem_limit_bytes=63 * 2**20
        ),
    )(
        trunk.reshape(rows, channels),
        conv_weight,
        head_weight,
        targets.reshape(rows, tracks),
        error_mask,
        upweight,
    )
    results = (conv_grad, head_grad, trunk_grad)
    conv_grad, head_grad, trunk_grad = pl.pallas_call(
        settle,
        out_shape=tuple(jax.ShapeDtypeStruct(r.shape, r.dtype) for r in results),
        in_specs=[away] * 3,
        out_specs=(away,) * 3,
        scratch_shapes=[pltpu.SemaphoreType.DMA((3,))],
        compiler_params=pltpu.CompilerParams(vmem_limit_bytes=63 * 2**20),
    )(*results)
    return loss.reshape(()), conv_grad, head_grad, trunk_grad.reshape(trunk.shape)


def fits(mesh):
    return mesh.shape["seq"] == 16 and mesh.shape["samp"] == 2


def solution(mesh):
    return jax.shard_map(
        per_device_kernel if fits(mesh) else per_device,
        mesh=mesh,
        in_specs=(
            P("samp", "seq", None),
            P(),
            P(),
            P("samp", "seq", None),
            P("samp", "seq"),
            P("samp", "seq"),
        ),
        out_specs=(P(), P(None, "seq", "samp"), P("seq", "samp"), P("samp", "seq", None)),
        check_vma=False,
    )
```

```python
import functools

import jax
import jax.numpy as jnp
from jax import lax
from jax.experimental import pallas as pl
from jax.experimental.pallas import tpu as pltpu
from jax.sharding import PartitionSpec as P

OUTPUT_TRACKS = 2688
LAYERS = 3
BASE_DILATION = 64


def extended(shard, width):
    devices, length = (lax.axis_size("seq"), shard.shape[1])
    up = [(i, (i + 1) % devices) for i in range(devices - 1)]
    down = [(j, i) for i, j in up]
    before = lax.ppermute(lax.slice_in_dim(shard, length - width, length, axis=1), "seq", up)
    after = lax.ppermute(lax.slice_in_dim(shard, 0, width, axis=1), "seq", down)
    return jnp.concatenate([before, shard, after], axis=1)


def smooth(values):
    return jax.nn.gelu(values, approximate=True)


def halve(part, dim, axis, bit):
    place = lax.axis_index(axis)
    mine = lax.rem(lax.div(place, 2**bit), 2)
    pairs = [(i, i ^ (2**bit)) for i in range(lax.axis_size(axis))]
    away = lax.dynamic_index_in_dim(part, 1 - mine, dim, keepdims=False)
    kept = lax.dynamic_index_in_dim(part, mine, dim, keepdims=False)
    come = lax.ppermute(away, axis, pairs)
    return (kept.astype(jnp.float32) + come.astype(jnp.float32)).astype(jnp.bfloat16)


def scatter_sum(part, order):
    labels = ["samp"] + list(reversed(range(part.ndim - 3)))
    for step in order:
        dim = labels.index(step)
        part = halve(part, dim, *(("samp", 0) if step == "samp" else ("seq", step)))
        labels.pop(dim)
    return part


def reduced(halves):
    devices = lax.axis_size("seq")
    bits = devices.bit_length() - 1
    rows = halves[0].shape[0] // devices
    stacked = jnp.stack([h.reshape((2,) * bits + (rows, h.shape[1])) for h in halves], axis=0)
    cut = max((rows * 5 // 9) // 16 * 16, 1)
    higher = list(range(2, bits))
    first = scatter_sum(stacked[..., :cut, :], [0, "samp", 1] + higher)
    second = scatter_sum(stacked[..., cut:, :], [0, 1, "samp"] + higher)
    return jnp.concatenate([first, second], axis=0).astype(jnp.float32)


def per_device(trunk, conv_weight, head_weight, targets, error_mask, upweight):
    windows, positions, channels = trunk.shape
    row_count = windows * positions
    bins_all = row_count * lax.axis_size("seq") * lax.axis_size("samp")
    bin_weight = jnp.where(error_mask == 1, upweight, 1).astype(jnp.float32)
    weight_sum = lax.psum(jnp.sum(bin_weight), ("seq", "samp"))
    stream = trunk
    stored = []
    padded_acts = []
    for layer_number in range(LAYERS):
        spread = BASE_DILATION * 2**layer_number
        activated = smooth(stream.astype(jnp.float32)).astype(jnp.bfloat16)
        padded = extended(activated, spread)
        taps = jnp.concatenate(
            [padded[:, k * spread : k * spread + positions] for k in range(3)], axis=2
        ).reshape(row_count, 3 * channels)
        conv_out = jnp.dot(
            taps,
            conv_weight[layer_number].reshape(3 * channels, channels),
            preferred_element_type=jnp.float32,
        )
        stored.append(stream)
        padded_acts.append(taps)
        stream = (stream.astype(jnp.float32) + conv_out.reshape(stream.shape)).astype(jnp.bfloat16)
    residual_rows = stream.reshape(row_count, channels)
    logits = jnp.dot(residual_rows, head_weight, preferred_element_type=jnp.float32)
    predicted = jax.nn.softplus(logits)
    slope = jax.nn.sigmoid(logits)
    counts = targets.reshape(row_count, -1).astype(jnp.float32)
    flat_weight = bin_weight.reshape(row_count, 1)
    partial_loss = jnp.sum(flat_weight * (predicted - counts * jnp.log(predicted)))
    loss_sum = lax.psum(partial_loss, ("seq", "samp"))
    factor = bins_all / weight_sum
    logit_grad = (factor * flat_weight * (1.0 - counts / predicted) * slope).astype(jnp.bfloat16)
    half = logit_grad.shape[1] // 2
    head_total = reduced(
        [
            jnp.dot(residual_rows.T, part, preferred_element_type=jnp.float32).astype(jnp.bfloat16)
            for part in (logit_grad[:, :half], logit_grad[:, half:])
        ]
    )
    stream_grad = jnp.dot(logit_grad, head_weight.T, preferred_element_type=jnp.float32).reshape(
        windows, positions, channels
    )
    kernel_grads = [None] * LAYERS
    for layer_number in reversed(range(LAYERS)):
        spread = BASE_DILATION * 2**layer_number
        grad_bf = stream_grad.astype(jnp.bfloat16)
        grad_flat = grad_bf.reshape(row_count, channels)
        padded_grad = extended(grad_bf, spread)
        side = channels // 2
        kernel_grads[layer_number] = reduced(
            [
                jnp.dot(
                    padded_acts[layer_number].T, part, preferred_element_type=jnp.float32
                ).astype(jnp.bfloat16)
                for part in (grad_flat[:, :side], grad_flat[:, side:])
            ]
        )
        act_grad = jnp.zeros((row_count, channels), jnp.float32)
        for k in range(3):
            view = padded_grad[:, (2 - k) * spread : (2 - k) * spread + positions]
            act_grad = act_grad + jnp.dot(
                view.reshape(row_count, channels),
                conv_weight[layer_number, k].T,
                preferred_element_type=jnp.float32,
            )
        residual_float32 = stored[layer_number].astype(jnp.float32)
        pullback = jax.vjp(smooth, residual_float32)[1]
        stream_grad = stream_grad + pullback(act_grad.reshape(residual_float32.shape))[0]
    loss = loss_sum / (OUTPUT_TRACKS * weight_sum)
    return (loss, jnp.stack(kernel_grads), head_total, stream_grad.astype(jnp.bfloat16))


MESH = pl.DeviceIdType.MESH
TILE = 384
ORDERS = (
    (("samp", 1, 2, 3), (1, "samp", 2, 3), (2, 3, "samp", 1)),
    ((1, 2, 3), (1, 2, 3), (1, 2, 3)),
    ((1, 2, 3), (2, 3, 1)),
    ((1, 2, 3), (2, 3, 1)),
)
LABELS = (("samp", 3, 2, 1), (3, 2, 1), (3, 2, 1), (3, 2, 1))
CUTS = ((0, 16, 32, 48), (0, 48, 96, 144), (0, 128, 144), (0, 80, 144))
CHUNKS = LAYERS + 1
TURNS = {
    0: (
    ),
    3: (
    ),
    2: (
        (0, 0, 0), (0, 1, 0), (0, 2, 0), (3, 1, 0), (3, 0, 0),
    ),
    1: (
        (2, 1, 0), (0, 1, 1), (0, 2, 1), (3, 1, 1), (2, 0, 0), (3, 0, 1),
        (2, 1, 1), (0, 2, 2), (0, 0, 1), (0, 1, 2), (1, 0, 0), (2, 0, 1),
        (3, 0, 2), (1, 1, 0), (0, 0, 2), (0, 1, 3), (1, 2, 0), (1, 0, 1),
        (3, 1, 2), (2, 1, 2), (0, 2, 3), (2, 0, 2), (1, 1, 1), (0, 0, 3),
        (1, 2, 1), (1, 0, 2), (1, 1, 2), (1, 2, 2),
    ),
}
SLOTS = tuple(
    (chunk, part, step)
    for chunk in range(CHUNKS)
    for part in range(len(ORDERS[chunk]))
    for step in range(len(LABELS[chunk]))
)
FIRST = 8 * LAYERS
LATER = FIRST + CHUNKS
LOSS = LATER + len(SLOTS)
COPIES = LOSS + 5


def smooth_slope(values):
    scale = 0.7978845608028654
    square = values * values
    bend = jnp.tanh(scale * values * (1.0 + 0.044715 * square))
    return 0.5 * (1.0 + bend) + 0.5 * values * (1.0 - bend * bend) * scale * (
        1.0 + 3 * 0.044715 * square
    )


def dot(left, right, left_dim, right_dim):
    return lax.dot_general(
        left, right, (((left_dim,), (right_dim,)), ((), ())), preferred_element_type=jnp.float32
    )


def kernel(
    trunk, conv_hbm, head_hbm, targets_hbm, mask, upweight, loss_out, conv_out, head_out, trunk_out, *scratch
):
    conv_w, head_w, counts, local_sem, send_sem, recv_sem, acts, grads, streams, slopes = scratch[:10]
    stream_grad, weights, sums, turned, other_acts, other_grads = scratch[10:16]
    scratch = scratch[5:]
    terms, first, later, loss_slots = (
        scratch[11 : 11 + CHUNKS],
        scratch[11 + CHUNKS : 11 + 2 * CHUNKS],
        scratch[11 + 2 * CHUNKS : -1],
        scratch[-1],
    )
    rows, channels = trunk.shape
    tracks = head_hbm.shape[1]
    seq, samp = lax.axis_index("seq"), lax.axis_index("samp")
    last = lax.axis_size("seq") - 1
    has_left, has_right = seq > 0, seq < last
    bits = [lax.rem(lax.div(seq, 2**b), 2) for b in range(4)]
    place = {"samp": samp, **{b: bits[b] for b in range(4)}}
    partner = {"samp": {"samp": 1 - samp}}
    for b in range(4):
        partner[b] = {"seq": seq + (1 - 2 * bits[b]) * 2**b}

    conv_loads = [
        pltpu.make_async_copy(conv_hbm.at[i], conv_w.at[i], local_sem.at[i]) for i in range(LAYERS)
    ]
    head_load = pltpu.make_async_copy(head_hbm, head_w, local_sem.at[LAYERS])
    count_load = pltpu.make_async_copy(targets_hbm, counts, local_sem.at[LAYERS + 1])
    for load in conv_loads + [head_load, count_load]:
        load.start()

    streams[0] = trunk[...]
    first_act = smooth(trunk[...].astype(jnp.float32)).astype(jnp.bfloat16)
    row = jnp.where(mask[...] == 1, upweight[...], 1).astype(jnp.float32)
    weights[...] = jnp.broadcast_to(row, (128, rows)).T

    barrier = pltpu.get_barrier_semaphore()
    right, left = {"seq": seq + 1}, {"seq": seq - 1}
    for there in (partner["samp"], partner[1], partner[2], partner[3]):
        pl.semaphore_signal(barrier, inc=1, device_id=there, device_id_type=MESH)

    @pl.when(has_right)
    def _():
        pl.semaphore_signal(barrier, inc=1, device_id=right, device_id_type=MESH)

    @pl.when(has_left)
    def _():
        pl.semaphore_signal(barrier, inc=1, device_id=left, device_id_type=MESH)

    pl.semaphore_wait(barrier, 4 + has_right.astype(jnp.int32) + has_left.astype(jnp.int32))

    def remote(src, dst, number, there):
        return pltpu.make_async_remote_copy(
            src_ref=src,
            dst_ref=dst,
            send_sem=send_sem.at[number],
            recv_sem=recv_sem.at[number],
            device_id=there,
            device_id_type=MESH,
        )

    spreads = [BASE_DILATION * 2**i for i in range(LAYERS)]
    starts = [sum(rows + 2 * s for s in spreads[:i]) for i in range(LAYERS)]

    def edges(buffer, layer, number):
        spread, start = spreads[layer], starts[layer]
        up = remote(
            buffer.at[pl.ds(start + rows, spread)], buffer.at[pl.ds(start, spread)], number, right
        )
        down = remote(
            buffer.at[pl.ds(start + spread, spread)],
            buffer.at[pl.ds(start + spread + rows, spread)],
            number + 1,
            left,
        )
        return up, down

    def send_edges(buffer, layer, number):
        spread, start = spreads[layer], starts[layer]
        up, down = edges(buffer, layer, number)

        @pl.when(has_right)
        def _():
            up.start()

        @pl.when(has_left)
        def _():
            down.start()

        @pl.when(jnp.logical_not(has_left))
        def _():
            buffer[pl.ds(start, spread)] = jnp.zeros((spread, channels), jnp.bfloat16)

        @pl.when(jnp.logical_not(has_right))
        def _():
            buffer[pl.ds(start + spread + rows, spread)] = jnp.zeros((spread, channels), jnp.bfloat16)

    def wait_edges(buffer, layer, number):
        up, down = edges(buffer, layer, number)

        @pl.when(has_right)
        def _():
            up.wait_send()
            down.wait_recv()

        @pl.when(has_left)
        def _():
            down.wait_send()
            up.wait_recv()

    def view(buffer, layer, tap):
        return buffer[pl.ds(starts[layer] + tap * spreads[layer], rows)]

    side = channels // 2
    my_side = pl.ds(pl.multiple_of(samp * side, 128), side)
    other_side = pl.ds(pl.multiple_of((1 - samp) * side, 128), side)

    def middle_rows(layer):
        return pl.ds(starts[layer] + spreads[layer], rows)

    def act_copy(layer):
        place_of = middle_rows(layer)
        return remote(
            acts.at[place_of], other_acts.at[place_of], 8 * layer + 6, partner["samp"]
        )

    def grad_copy(layer):
        return remote(
            grads.at[middle_rows(layer), other_side],
            other_grads.at[layer],
            8 * layer + 7,
            partner["samp"],
        )

    for layer in range(LAYERS):
        block = first_act
        if layer > 0:
            block = smooth(streams[layer].astype(jnp.float32)).astype(jnp.bfloat16)
        acts[middle_rows(layer)] = block
        send_edges(acts, layer, 8 * layer)
        act_copy(layer).start()
        conv_loads[layer].wait()
        total = streams[layer].astype(jnp.float32) + dot(view(acts, layer, 1), conv_w[layer, 1], 1, 0)
        wait_edges(acts, layer, 8 * layer)
        for tap in (0, 2):
            total += dot(view(acts, layer, tap), conv_w[layer, tap], 1, 0)
        streams[layer + 1] = total.astype(jnp.bfloat16)

    for layer in reversed(range(LAYERS)):
        act_copy(layer).wait()
        send_edges(other_acts, layer, 8 * layer + 2)

    head_load.wait()
    count_load.wait()
    turned[...] = streams[LAYERS][...].T

    def folded(values):
        return jnp.sum(values.reshape(rows // 8, 8, values.shape[1]), axis=0)

    def first_copy(chunk):
        return remote(
            terms[chunk].at[(slice(None),) * len(LABELS[chunk]) + (1 - bits[0],)],
            first[chunk],
            FIRST + chunk,
            partner[0],
        )

    def part_rows(chunk, part):
        return pl.ds(CUTS[chunk][part], CUTS[chunk][part + 1] - CUTS[chunk][part])

    def slot(chunk, part, step):
        return later[SLOTS.index((chunk, part, step))]

    def picked(chunk, part, step, which):
        order = ORDERS[chunk][part]
        labels = list(LABELS[chunk])
        for done in order[:step]:
            labels.remove(done)
        dim = labels.index(order[step])
        index = place[order[step]] if which == 0 else 1 - place[order[step]]
        return labels, dim, index

    def later_copy(chunk, part, step):
        labels, dim, index = picked(chunk, part, step, 1)
        at = [slice(None)] * len(labels)
        at[dim] = index
        if step == 0:
            src = first[chunk].at[tuple(at) + (part_rows(chunk, part),)]
        else:
            src = slot(chunk, part, step - 1).at[tuple(at)]
        number = LATER + SLOTS.index((chunk, part, step))
        return remote(src, slot(chunk, part, step), number, partner[ORDERS[chunk][part][step]])

    def added(a, b):
        return a.astype(jnp.float32) + b.astype(jnp.float32)

    def digits(number, count):
        return tuple(lax.rem(lax.div(number, 2 ** (count - 1 - i)), 2) for i in range(count))

    def start_later(chunk):
        first_copy(chunk).wait()

        def add(number, carry):
            at = digits(number, len(LABELS[chunk]))
            first[chunk][at] = added(first[chunk][at], terms[chunk][at + (bits[0],)]).astype(
                jnp.bfloat16
            )
            return carry

        lax.fori_loop(0, 2 ** len(LABELS[chunk]), add, 0)
        for part in range(len(ORDERS[chunk])):
            later_copy(chunk, part, 0).start()

    def advance(chunk, part, step):
        later_copy(chunk, part, step).wait()
        labels, dim, index = picked(chunk, part, step, 0)
        held = slot(chunk, part, step)
        before = first[chunk] if step == 0 else slot(chunk, part, step - 1)
        count = len(labels) - 1

        def values(at):
            there = at[:dim] + (index,) + at[dim:]
            if step == 0:
                there = there + (part_rows(chunk, part),)
            return added(held[at] if at else held[...], before[there])

        if step == len(LABELS[chunk]) - 1:
            where = part_rows(chunk, part)
            total = values(()) * factor()
            if chunk == 0:
                half = head_out.shape[1]
                moved = pltpu.roll(total, half, axis=1)
                head_out[where] = jnp.where(samp == 1, moved, total)[:, :half]
            else:
                conv_out[chunk - 1, where] = total
        else:

            def add(number, carry):
                at = digits(number, count)
                held[at] = values(at).astype(jnp.bfloat16)
                return carry

            lax.fori_loop(0, 2**count, add, 0)
            later_copy(chunk, part, step + 1).start()

    def weight_sum():
        return jnp.sum(sums[8:16, 0:1], axis=0, keepdims=True)

    def factor():
        bins_all = float(rows) * lax.axis_size("seq") * lax.axis_size("samp")
        return bins_all / weight_sum()

    def loss_copy(step):
        there = partner[(0, "samp", 1, 2, 3)[step]]
        return remote(loss_slots.at[2 * step], loss_slots.at[2 * step + 1], LOSS + step, there)

    def loss_start(step):
        loss_slots[2 * step] = sums[...]
        loss_copy(step).start()

    def loss_end(step):
        loss_copy(step).wait()
        sums[...] += loss_slots[2 * step + 1]

    def put(chunk, value, row):
        size = terms[chunk].shape[4]
        at = 0
        while at < value.shape[0]:
            block, inner = divmod(row + at, size)
            length = min(size - inner, value.shape[0] - at)
            where = tuple((block >> b) & 1 for b in (3, 2, 1, 0))
            terms[chunk][where + (pl.ds(inner, length),)] = value[at : at + length].astype(jnp.bfloat16)
            at += length

    wide = terms[0].shape[6]
    loss_fold = jnp.zeros((8, 128), jnp.float32)
    for tile in range(tracks // TILE):
        begin = tile * TILE
        matrix = head_w[:, begin : begin + TILE]
        logits = dot(streams[LAYERS], matrix, 1, 0)
        weight = jnp.concatenate([weights[...]] * (TILE // 128), axis=1)
        tail = jnp.exp(-jnp.abs(logits))
        above = 1.0 + tail
        inverse = 1.0 / above
        predicted = jnp.maximum(logits, 0.0) + (jnp.log(above) + (tail - (above - 1.0)) * inverse)
        slope = jnp.where(logits >= 0, 1.0, tail) * inverse
        seen = counts[:, begin : begin + TILE].astype(jnp.float32)
        fold = folded(weight * (predicted - seen * jnp.log(predicted)))
        loss_fold += sum(fold[:, i * 128 : (i + 1) * 128] for i in range(TILE // 128))
        grad = (weight * (1.0 - seen / predicted) * slope).astype(jnp.bfloat16)
        slopes[:, begin : begin + TILE] = grad
        value = dot(turned[...], grad, 1, 0).astype(jnp.bfloat16)
        for side in range(2):
            base = side * (tracks - wide)
            low, high = max(begin, base), min(begin + TILE, base + wide)
            if low < high:
                for block in range(16):
                    where = (side,) + tuple((block >> b) & 1 for b in (3, 2, 1, 0))
                    terms[0][where + (slice(None), pl.ds(low - base, high - low))] = value[
                        block * 48 : (block + 1) * 48, low - begin : high - begin
                    ]
    first_copy(0).start()
    sums[0:8] = loss_fold
    sums[8:16] = folded(weights[...])
    loss_start(0)
    stream_grad[...] = dot(slopes[...], head_w[...], 1, 1)

    def send_grad(layer):
        grads[middle_rows(layer)] = stream_grad[...].astype(jnp.bfloat16)
        send_edges(grads, layer, 8 * layer + 4)
        grad_copy(layer).start()

    def begin_and_turn(chunk):
        start_later(chunk)
        for turn in TURNS[chunk]:
            advance(*turn)

    send_grad(LAYERS - 1)
    chunk = 0
    for layer in reversed(range(LAYERS)):
        total = dot(view(grads, layer, 1), conv_w[layer, 1], 1, 1)
        begin_and_turn(chunk)
        chunk = layer + 1
        wait_edges(grads, layer, 8 * layer + 4)
        for tap in (0, 2):
            total += dot(view(grads, layer, 2 - tap), conv_w[layer, tap], 1, 1)
        stream_grad[...] += smooth_slope(streams[layer].astype(jnp.float32)) * total
        if layer > 0:
            send_grad(layer - 1)
        loss_end(LAYERS - 1 - layer)
        loss_start(LAYERS - layer)
        wait_edges(other_acts, layer, 8 * layer + 2)
        grad_copy(layer).wait()
        both = jnp.concatenate([grads[middle_rows(layer), my_side], other_grads[layer]], axis=0)
        for tap in range(3):
            place_of = pl.ds(starts[layer] + tap * spreads[layer], rows)
            for begin in range(0, channels, 384):
                seen = jnp.concatenate(
                    [
                        acts[place_of, begin : begin + 384],
                        other_acts[place_of, begin : begin + 384],
                    ],
                    axis=0,
                )
                put(layer + 1, dot(seen, both, 0, 0), tap * channels + begin)
        first_copy(layer + 1).start()
    loss_end(3)
    loss_start(4)
    start_later(1)
    loss_end(4)
    trunk_out[...] = (stream_grad[...] * factor()).astype(jnp.bfloat16)
    loss_out[...] = jnp.sum(
        jnp.sum(sums[0:8], axis=0, keepdims=True), axis=1, keepdims=True
    ) / (OUTPUT_TRACKS * weight_sum())
    for turn in TURNS[1]:
        advance(*turn)


def per_device_kernel(trunk, conv_weight, head_weight, targets, error_mask, upweight):
    windows, rows, channels = trunk.shape
    devices = lax.axis_size("seq")
    tracks = head_weight.shape[1]
    spreads = [BASE_DILATION * 2**i for i in range(LAYERS)]
    extended_rows = sum(rows + 2 * s for s in spreads)
    half = tracks // 2
    wide = (half + 127) // 128 * 128
    sizes = [(channels // devices, wide)] + [(3 * channels // devices, channels // 2)] * LAYERS
    vmem = functools.partial(pltpu.VMEM, dtype=jnp.bfloat16)
    scratch = [
        vmem(conv_weight.shape),
        vmem(head_weight.shape),
        pltpu.VMEM((rows, tracks), jnp.int32),
        pltpu.SemaphoreType.DMA((LAYERS + 2,)),
        pltpu.SemaphoreType.DMA((COPIES,)),
        pltpu.SemaphoreType.DMA((COPIES,)),
        vmem((extended_rows, channels)),
        vmem((extended_rows, channels)),
        vmem((LAYERS + 1, rows, channels)),
        vmem((rows, tracks)),
        pltpu.VMEM((rows, channels), jnp.float32),
        pltpu.VMEM((rows, 128), jnp.float32),
        pltpu.VMEM((16, 128), jnp.float32),
        vmem((channels, rows)),
        vmem((extended_rows, channels)),
        vmem((LAYERS, rows, channels // 2)),
    ]
    counts = [len(labels) for labels in LABELS]
    scratch += [vmem((2,) * (count + 1) + size) for count, size in zip(counts, sizes)]
    scratch += [vmem((2,) * count + size) for count, size in zip(counts, sizes)]
    for chunk, part, step in SLOTS:
        part_rows = CUTS[chunk][part + 1] - CUTS[chunk][part]
        scratch.append(vmem((2,) * (counts[chunk] - 1 - step) + (part_rows, sizes[chunk][1])))
    scratch.append(pltpu.VMEM((10, 16, 128), jnp.float32))
    whole = pl.BlockSpec(memory_space=pltpu.VMEM)
    away = pl.BlockSpec(memory_space=pl.ANY)
    loss, conv_grad, head_grad, trunk_grad = pl.pallas_call(
        kernel,
        out_shape=(
            jax.ShapeDtypeStruct((1, 1), jnp.float32),
            jax.ShapeDtypeStruct((LAYERS,) + sizes[1], jnp.float32),
            jax.ShapeDtypeStruct((sizes[0][0], half), jnp.float32),
            jax.ShapeDtypeStruct((rows, channels), jnp.bfloat16),
        ),
        in_specs=[whole, away, away, away, whole, whole],
        out_specs=(whole,) * 4,
        scratch_shapes=scratch,
        compiler_params=pltpu.CompilerParams(
            collective_id=0, has_side_effects=True, vmem_limit_bytes=63 * 2**20
        ),
    )(
        trunk.reshape(rows, channels),
        conv_weight,
        head_weight,
        targets.reshape(rows, tracks),
        error_mask,
        upweight,
    )
    return loss.reshape(()), conv_grad, head_grad, trunk_grad.reshape(trunk.shape)


def fits(mesh):
    return mesh.shape["seq"] == 16 and mesh.shape["samp"] == 2


def solution(mesh):
    return jax.shard_map(
        per_device_kernel if fits(mesh) else per_device,
        mesh=mesh,
        in_specs=(
            P("samp", "seq", None),
            P(),
            P(),
            P("samp", "seq", None),
            P("samp", "seq"),
            P("samp", "seq"),
        ),
        out_specs=(P(), P(None, "seq", "samp"), P("seq", "samp"), P("samp", "seq", None)),
        check_vma=False,
    )
```
